32 devices in a mesh: leaf: 8 (over z, x), grp: 4 (over y, core).
Axes of the slice: x: 2, y: 2, z: 4, core: 2. Of those that a mesh axis runs over, the one named last changes fastest.
Arguments:
- hidden_states: bfloat16 [4, 1024, 2560], P('grp', 'leaf'), may hold values from -6 to 6
- query_rows: bfloat16 [4, 1024, 5120], P('grp', 'leaf'), may hold values from -170 to 170
- key_rows: bfloat16 [4, 1024, 512], P('grp', 'leaf'), may hold values from -7 to 7
- value_weight: bfloat16 [2560, 512], P(('leaf', 'grp')), may hold values from -0.125 to 0.125
- parent_links: int32 [4, 8], P('grp', 'leaf'), may hold values from -1 to 6, as said below
- out_grad: bfloat16 [4, 1024, 5120], P('grp', 'leaf'), may hold values from -6 to 6
Outputs:
- attended: bfloat16 [4, 1024, 5120], P('grp', 'leaf')
- query_grad: bfloat16 [4, 1024, 5120], P('grp', 'leaf')
- key_grad: bfloat16 [4, 1024, 512], P('grp', 'leaf')
- hidden_grad: bfloat16 [4, 1024, 2560], P('grp', 'leaf')
- weight_grad: float32 [2560, 512], P(('leaf', 'grp'))
The draws below stay inside these ranges and needn't reach their ends.
Inputs may be any that keep to these rules, and one draw needn't show every extreme that they name: `parent_links`: entry 0 of each tree is -1 and every other entry names a lower index; no segment has more than 4 children, every segment is at most 3 steps from segment 0, and in every tree some segment is exactly 3 steps from it and segment 0 has exactly 4 children.
All inputs are finite; a program needn't handle non-finite values.
Results may differ from the reference program's by a relative error of at most 0.028.
Values may be sent and summed in bfloat16 or wider, within the bound.
A program may use at most 128 MiB of HBM per device.

```python
import jax
import jax.numpy as jnp
from jax import lax

D = 2560
HQ = 40
HK = 4
DH = 128
SEG = 128
TOKENS = 1024
N_LEAF = 8
N_GRP = 4


def shared_keys(key):
    return jnp.clip(jax.random.normal(key, (N_GRP, N_LEAF * SEG, HK * DH), jnp.float32), -6.0, 6.0)


def draw_key_rows(key, part):
    base_rows = shared_keys(key)
    return base_rows.astype(jnp.bfloat16)


def draw_query_rows(key, part):
    key = jax.random.fold_in(key, 5)
    fresh_rows = jnp.clip(jax.random.normal(key, (N_GRP, N_LEAF * SEG, HQ * DH), jnp.float32), -6.0, 6.0)
    return fresh_rows.astype(jnp.bfloat16)


def build_tree(key):
    node_ids = jnp.arange(N_LEAF, dtype=jnp.int32)
    ranking = jax.random.randint(key, (N_LEAF, N_LEAF), 0, 65536, dtype=jnp.int32) * 128 + node_ids[None, :]
    first_pick = jax.random.randint(jax.random.fold_in(key, 2), (), 1, 5, dtype=jnp.int32)
    parent_of = jnp.where((node_ids >= 1) & (node_ids <= 4), 0, -1).astype(jnp.int32)
    parent_of = parent_of.at[5].set(first_pick).at[6].set(5)
    depth_of = jnp.where(node_ids == 0, 0, jnp.where(node_ids <= 4, 1, jnp.where(node_ids == 5, 2, jnp.where(node_ids == 6, 3, 9)))).astype(jnp.int32)
    child_count = jnp.zeros((N_LEAF,), jnp.int32).at[0].set(4).at[first_pick].add(1).at[5].add(1)

    def step(node_index, carry):
        parent_now, depth_now, count_now = carry
        eligible = (node_ids < node_index) & (depth_now >= 1) & (depth_now <= 2) & (count_now < 4)
        ranked = jnp.where(eligible, ranking[node_index], -1)
        chosen = jnp.argmax(ranked).astype(jnp.int32)
        return (parent_now.at[node_index].set(chosen), depth_now.at[node_index].set(depth_now[chosen] + 1), count_now.at[chosen].add(1))
    parent_of, depth_of, child_count = lax.fori_loop(7, N_LEAF, step, (parent_of, depth_of, child_count))
    return parent_of.astype(jnp.int32)


def draw_parent_links(key, part):
    key = jax.random.fold_in(key, 11)
    return jax.vmap(build_tree)(jax.random.split(key, N_GRP))


def spiked(array, key, source, target, parts, factor):
    owner, partner = [(jnp.arange(array.shape[dim]) // (array.shape[dim] // parts)).reshape([-1 if axis == dim else 1 for axis in range(array.ndim)]) for dim in (source, target)]
    chosen = jax.random.permutation(key, parts)[partner]
    strong = (owner == chosen) | (owner == (partner + parts // 2) % parts)
    return jnp.where(strong, factor * array, array)


def block_scale(own_key, shape, shards, smallest, largest):
    factor_of, own = 1.0, jax.random.fold_in(own_key, 6)
    for position, shards_of in shards:
        steps = jnp.exp(jax.random.uniform(jax.random.fold_in(own, position), (shards_of,), jnp.float32, smallest / len(shards), largest / len(shards)))
        factor_of = factor_of * jnp.repeat(steps, shape[position] // shards_of).reshape([-1 if axis == position else 1 for axis in range(len(shape))])
    return factor_of


def normal_values(key, dims, spread, reach, cuts=(), kind=jnp.bfloat16):
    gain = block_scale(key, dims, cuts, -0.22, 0.18) if cuts else 1.0
    drawn = jax.random.normal(key, dims, jnp.float32) * spread * gain
    return jnp.minimum(jnp.maximum(drawn, -reach), reach).astype(kind)


def heavy_noise(own_key, dims, spread, bound, pieces, heavy, held_as=jnp.bfloat16):
    drawn = spread * jax.random.normal(own_key, dims, jnp.float32)
    if pieces:
        drawn = drawn * block_scale(own_key, dims, pieces, -0.22, 0.18)
    return jnp.clip(spiked(drawn, jax.random.fold_in(own_key, 3), *heavy), -bound, bound).astype(held_as)


def setup_inputs(seed: int = 0) -> dict:
    streams_of = jax.random.split(jax.random.key(seed), 7)
    return {
        "hidden_states": heavy_noise(streams_of[0], (N_GRP, TOKENS, D), 1.0, 6.0, ((0, 4), (1, 8)), (1, 2, 8, 2.0)),
        "query_rows": draw_query_rows(jax.random.fold_in(streams_of[6], 71), 0),
        "key_rows": draw_key_rows(jax.random.fold_in(streams_of[6], 71), 0),
        "value_weight": normal_values(streams_of[3], (D, HK * DH), D ** -0.5, 0.125, ((0, 32),)),
        "parent_links": draw_parent_links(jax.random.fold_in(streams_of[6], 71), 0),
        "out_grad": normal_values(streams_of[5], (N_GRP, TOKENS, HQ * DH), 1.0, 6.0, ((0, 4), (1, 8))),
    }


def chain_slots(parent_list, own_index):
    total = parent_list.shape[0]

    def parent_of(node_index):
        hit = jnp.arange(total, dtype=jnp.int32) == node_index
        found = jnp.sum(jnp.where(hit, parent_list, 0)).astype(jnp.int32)
        return jnp.where(node_index >= 0, found, -1).astype(jnp.int32)

    first = parent_of(own_index)
    second = parent_of(first)
    third = parent_of(second)
    return jnp.stack([first, second, third]).astype(jnp.int32)


def key_mask(ancestors, segment_len):
    valid = jnp.concatenate([ancestors >= 0, jnp.ones((1,), bool)])
    block_ok = jnp.repeat(valid, segment_len)[None, :]
    row_ids = jnp.arange(segment_len, dtype=jnp.int32)[:, None]
    col_ids = jnp.arange(4 * segment_len, dtype=jnp.int32)[None, :]
    causal = (col_ids < 3 * segment_len) | (col_ids - 3 * segment_len <= row_ids)
    return block_ok & causal


def segment_pass(query_seg, key_all, value_all, grad_seg, visible):
    segment_len = query_seg.shape[0]
    groups = HQ // HK
    scale_factor = 1.0 / (DH ** 0.5)
    query_heads = query_seg.astype(jnp.float32).reshape(segment_len, HK, groups, DH)
    key_heads = key_all.astype(jnp.float32).reshape(-1, HK, DH)
    value_heads = value_all.astype(jnp.float32).reshape(-1, HK, DH)
    grad_heads = grad_seg.astype(jnp.float32).reshape(segment_len, HK, groups, DH)
    scores = jnp.einsum('rhgd,khd->hgrk', query_heads, key_heads) * scale_factor
    scores = jnp.where(visible, scores, -1e30)
    row_max = jnp.max(scores, axis=-1, keepdims=True)
    weights_exp = jnp.where(visible, jnp.exp(scores - row_max), 0.0)
    probs = weights_exp / jnp.sum(weights_exp, axis=-1, keepdims=True)
    probs_low = probs.astype(jnp.bfloat16).astype(jnp.float32)
    output = jnp.einsum('hgrk,khd->rhgd', probs_low, value_heads).reshape(segment_len, HQ * DH).astype(jnp.bfloat16)
    dprobs = jnp.einsum('rhgd,khd->hgrk', grad_heads, value_heads)
    delta = jnp.sum(probs * dprobs, axis=-1, keepdims=True)
    dscores = (probs * (dprobs - delta)).astype(jnp.bfloat16).astype(jnp.float32)
    query_grad = (jnp.einsum('hgrk,khd->rhgd', dscores, key_heads) * scale_factor).reshape(segment_len, HQ * DH).astype(jnp.bfloat16)
    key_part = jnp.einsum('hgrk,rhgd->khd', dscores, query_heads) * scale_factor
    value_part = jnp.einsum('hgrk,rhgd->khd', probs_low, grad_heads)
    grad_term = jnp.concatenate([key_part.reshape(-1, HK * DH), value_part.reshape(-1, HK * DH)], axis=1)
    return output, query_grad, grad_term


def reference(hidden_states, query_rows, key_rows, value_weight, parent_links, out_grad):
    key_width = HK * DH

    def one_group(inputs):
        hidden_g, query_g, key_g, parent_g, grad_g = inputs
        values = jnp.dot(hidden_g, value_weight, preferred_element_type=jnp.float32).astype(jnp.bfloat16)
        key_value = jnp.concatenate([key_g, values], axis=1)

        def step(carry, seg_index):
            ancestors = chain_slots(parent_g, seg_index)
            blocks = [lax.dynamic_slice_in_dim(key_value, (jnp.maximum(ancestors[i], 0) * SEG).astype(jnp.int32), SEG, 0) for i in range(3)]
            own_start = (seg_index * SEG).astype(jnp.int32)
            blocks.append(lax.dynamic_slice_in_dim(key_value, own_start, SEG, 0))
            gathered = jnp.concatenate(blocks, axis=0)
            query_seg = lax.dynamic_slice_in_dim(query_g, own_start, SEG, 0)
            grad_seg = lax.dynamic_slice_in_dim(grad_g, own_start, SEG, 0)
            output, query_grad, grad_term = segment_pass(query_seg, gathered[:, :key_width], gathered[:, key_width:], grad_seg, key_mask(ancestors, SEG))
            term_low = lax.optimization_barrier(grad_term.astype(jnp.bfloat16)).astype(jnp.float32)
            owners = jnp.concatenate([ancestors, seg_index[None]]).astype(jnp.int32)
            for slot_index in range(4):
                start = (jnp.maximum(owners[slot_index], 0) * SEG).astype(jnp.int32)
                current = lax.dynamic_slice_in_dim(carry, start, SEG, 0)
                carry = lax.dynamic_update_slice_in_dim(carry, current + term_low[slot_index * SEG:(slot_index + 1) * SEG], start, 0)
            return carry, (output, query_grad)

        sums, (outputs, query_grads) = lax.scan(step, jnp.zeros((N_LEAF * SEG, 2 * key_width), jnp.float32), jnp.arange(N_LEAF, dtype=jnp.int32))
        key_grad = sums[:, :key_width].astype(jnp.bfloat16)
        value_grad = sums[:, key_width:].astype(jnp.bfloat16)
        hidden_grad = jnp.dot(value_grad, value_weight.T, preferred_element_type=jnp.float32).astype(jnp.bfloat16)
        weight_part = jnp.dot(hidden_g.T, value_grad, preferred_element_type=jnp.float32)
        return outputs.reshape(N_LEAF * SEG, HQ * DH), query_grads.reshape(N_LEAF * SEG, HQ * DH), key_grad, hidden_grad, weight_part

    results = lax.map(one_group, (hidden_states, query_rows, key_rows, parent_links, out_grad))
    weight_grad = jnp.sum(results[4], axis=0)
    return results[0], results[1], results[2], results[3], weight_grad
```

```python
import functools

import jax
import jax.numpy as jnp
from jax import lax
from jax.experimental import pallas as pl
from jax.experimental.pallas import tpu as pltpu
from jax.sharding import PartitionSpec as P

HQ = 40
HK = 4
DH = 128
MESH = pl.DeviceIdType.MESH
NX = 2
NC = 2
VMEM_LIMIT = 56 * 1024 * 1024


def nt(a, b):
    return lax.dot_general(a, b, (((1,), (1,)), ((), ())), preferred_element_type=jnp.float32)


def nn(a, b):
    return jnp.dot(a, b, preferred_element_type=jnp.float32)


def place():
    leaf = lax.axis_index("leaf")
    grp = lax.axis_index("grp")
    return leaf, grp, leaf // NX, leaf % NX, grp // NC, grp % NC


def remote(src, dst, send, recv, leaf, grp):
    return pltpu.make_async_remote_copy(
        src_ref=src,
        dst_ref=dst,
        send_sem=send,
        recv_sem=recv,
        device_id=(leaf, grp),
        device_id_type=MESH,
    )


def greet(leaf, grp, n_leaf, n_grp):
    barrier = pltpu.get_barrier_semaphore()
    for step in range(1, n_leaf):
        pl.semaphore_signal(
            barrier, inc=1, device_id=(lax.rem(leaf + step, n_leaf), grp), device_id_type=MESH
        )
    for step in range(1, n_grp):
        pl.semaphore_signal(
            barrier, inc=1, device_id=(leaf, lax.rem(grp + step, n_grp)), device_id_type=MESH
        )
    pl.semaphore_wait(barrier, n_leaf + n_grp - 2)


def gather_kernel(
    n_leaf, n_grp,
    parent_ref, w_ref, key_ref, hidden_ref,
    w_all, key_all, value_all, parents,
    own_parent, par_send, par_recv, wz_send, wz_recv, w_send, w_recv, c_send, c_recv,
    kz_send, kz_recv, kx_send, kx_recv, vz_send, vz_recv, vx_send, vx_recv,
):
    leaf, grp, z, x, y, c = place()
    nz = n_leaf // NX
    x_peer, y_peer, c_peer = z * NX + (1 - x), (1 - y) * NC + c, y * NC + (1 - c)
    half = w_ref.shape[1] // 2
    low, high = pl.ds(0, half), pl.ds(half, half)
    pending = []

    own_parent[...] = jnp.full(own_parent.shape, parent_ref[0, 0], jnp.int32)
    greet(leaf, grp, n_leaf, n_grp)

    def start(copy):
        copy.start()
        pending.append(copy)
        return copy

    wz = []
    for d in range(1, nz):
        to = lax.rem(z + d, nz)
        wz.append(
            start(remote(w_ref, w_all.at[z, x, y, c], wz_send.at[d - 1], wz_recv.at[d - 1], to * NX + x, grp))
        )
    par = []
    for d in range(1, n_leaf):
        par.append(
            start(
                remote(
                    own_parent, parents.at[leaf], par_send.at[d - 1], par_recv.at[d - 1],
                    lax.rem(leaf + d, n_leaf), grp,
                )
            )
        )
    w_all[z, x, y, c] = w_ref[...]
    key_all[leaf] = key_ref[...]
    parents[leaf] = own_parent[...]

    def up_copy(block, whole, sems, d):
        return remote(block, whole.at[leaf], sems[0].at[d - 1], sems[1].at[d - 1], leaf + d * NX, grp)

    def up_start(block, whole, sems):
        for d in range(1, nz):
            @pl.when(z + d < nz)
            def _(d=d):
                up_copy(block, whole, sems, d).start()

    def across_copy(whole, sems, d):
        slot = leaf - d * NX
        return remote(whole.at[slot], whole.at[slot], sems[0].at[d], sems[1].at[d], x_peer, grp)

    def across_own(block, whole, sems):
        @pl.when(x == 0)
        def _():
            remote(block, whole.at[leaf], sems[0].at[0], sems[1].at[0], x_peer, grp).start()

    def across_start(whole, up_sems, sems):
        for d in range(1, nz):
            @pl.when(z - d >= 0)
            def _(d=d):
                slot = leaf - d * NX
                remote(whole.at[slot], whole.at[slot], up_sems[0].at[d - 1], up_sems[1].at[d - 1], leaf, grp).wait_recv()
                across_copy(whole, sems, d).start()

    def finish(block, whole, up_sems, sems):
        for d in range(1, nz):
            @pl.when(z - d >= 0)
            def _(d=d):
                slot = z * NX - d * NX + (1 - x)
                remote(whole.at[slot], whole.at[slot], sems[0].at[d], sems[1].at[d], x_peer, grp).wait()

            @pl.when(z + d < nz)
            def _(d=d):
                up_copy(block, whole, up_sems, d).wait_send()

        @pl.when(x == 0)
        def _():
            remote(block, whole.at[leaf], sems[0].at[0], sems[1].at[0], x_peer, grp).wait_send()

        @pl.when(x == 1)
        def _():
            remote(block, whole.at[x_peer], sems[0].at[0], sems[1].at[0], x_peer, grp).wait_recv()

    for copy in wz:
        copy.wait_recv()

    column_a = w_all.at[:, x, y, c, :, low]
    column_b = w_all.at[:, x, y, c, :, high]
    first_a = start(remote(column_a, column_a, w_send.at[0], w_recv.at[0], x_peer, grp))
    first_b = start(remote(column_b, column_b, w_send.at[1], w_recv.at[1], leaf, y_peer))
    whole_c = w_all.at[:, x, y, c]
    to_core = [start(remote(whole_c, whole_c, c_send.at[0], c_recv.at[0], leaf, c_peer))]
    up_start(key_ref, key_all, (kz_send, kz_recv))

    first_a.wait_recv()
    plane_a = w_all.at[:, :, y, c, :, low]
    second_a = start(remote(plane_a, plane_a, w_send.at[2], w_recv.at[2], leaf, y_peer))
    first_b.wait_recv()
    plane_b = w_all.at[:, x, :, c, :, high]
    second_b = start(remote(plane_b, plane_b, w_send.at[3], w_recv.at[3], x_peer, grp))
    got_a = w_all.at[:, 1 - x, y, c, :, low]
    got_b = w_all.at[:, x, 1 - y, c, :, high]
    to_core.append(start(remote(got_a, got_a, c_send.at[1], c_recv.at[1], leaf, c_peer)))
    to_core.append(start(remote(got_b, got_b, c_send.at[2], c_recv.at[2], leaf, c_peer)))

    second_a.wait_recv()
    late_a = w_all.at[:, :, 1 - y, c, :, low]
    to_core.append(start(remote(late_a, late_a, c_send.at[3], c_recv.at[3], leaf, c_peer)))
    second_b.wait_recv()
    late_b = w_all.at[:, 1 - x, :, c, :, high]
    to_core.append(start(remote(late_b, late_b, c_send.at[4], c_recv.at[4], leaf, c_peer)))
    across_own(key_ref, key_all, (kx_send, kx_recv))
    across_start(key_all, (kz_send, kz_recv), (kx_send, kx_recv))
    for copy in to_core:
        copy.wait_recv()

    weight = w_all[...].reshape(hidden_ref.shape[1], w_ref.shape[1])
    value_all[leaf] = nn(hidden_ref[...], weight).astype(jnp.bfloat16)
    value_own = value_all.at[leaf]
    up_start(value_own, value_all, (vz_send, vz_recv))
    across_own(value_own, value_all, (vx_send, vx_recv))
    across_start(value_all, (vz_send, vz_recv), (vx_send, vx_recv))

    finish(key_ref, key_all, (kz_send, kz_recv), (kx_send, kx_recv))
    for copy in par:
        copy.wait_recv()
    finish(value_own, value_all, (vz_send, vz_recv), (vx_send, vx_recv))
    for copy in pending:
        copy.wait_send()


def gather_call(parent, w, key, hidden, n_leaf, n_grp):
    nz, ny = n_leaf // NX, n_grp // NC
    vmem = pl.BlockSpec(memory_space=pltpu.VMEM)
    dma = pltpu.SemaphoreType.DMA
    return pl.pallas_call(
        functools.partial(gather_kernel, n_leaf, n_grp),
        out_shape=[
            jax.ShapeDtypeStruct((nz, NX, ny, NC) + w.shape, w.dtype),
            jax.ShapeDtypeStruct((n_leaf,) + key.shape, key.dtype),
            jax.ShapeDtypeStruct((n_leaf,) + key.shape, key.dtype),
            jax.ShapeDtypeStruct((n_leaf, 8, 128), jnp.int32),
        ],
        in_specs=[pl.BlockSpec(memory_space=pltpu.SMEM)] + [vmem] * 3,
        out_specs=[vmem] * 4,
        scratch_shapes=[pltpu.VMEM((8, 128), jnp.int32)]
        + [dma((n_leaf - 1,))] * 2
        + [dma((nz - 1,))] * 2
        + [dma((4,))] * 2
        + [dma((5,))] * 2
        + ([dma((nz - 1,))] * 2 + [dma((nz,))] * 2) * 2,
        compiler_params=pltpu.CompilerParams(
            collective_id=0, has_side_effects=True, vmem_limit_bytes=VMEM_LIMIT
        ),
        cost_estimate=pl.CostEstimate(flops=2 * 128 * 2560 * 512, bytes_accessed=6000000, transcendentals=0),
    )(parent, w, key, hidden)


def ancestors_of(par, own):
    first = par[own]
    second = jnp.where(first >= 0, par[jnp.maximum(first, 0)], -1)
    third = jnp.where(second >= 0, par[jnp.maximum(second, 0)], -1)
    return first, second, third


def attention_kernel(
    par, own, q_ref, g_ref, k0, k1, k2, k3, v0, v1, v2, v3,
    o_ref, dq_ref, dk_ref, dv_ref, bias,
):
    seg = q_ref.shape[0]
    groups = HQ // HK
    scale = 1.0 / DH**0.5
    fold = scale * 1.4426950408889634
    chain = ancestors_of(par, own[0])

    @pl.when(pl.program_id(0) == 0)
    def _():
        for i in range(3):
            bias[i * seg : (i + 1) * seg, :] = jnp.full(
                (seg, 2 * seg), jnp.where(chain[i] >= 0, 0.0, -1e30), jnp.float32
            )
        col = lax.broadcasted_iota(jnp.int32, (seg, 2 * seg), 0)
        row = lax.broadcasted_iota(jnp.int32, (seg, 2 * seg), 1)
        row = jnp.where(row >= seg, row - seg, row)
        bias[3 * seg :, :] = jnp.where(col <= row, 0.0, -1e30)

    key = jnp.concatenate([k0[0], k1[0], k2[0], k3[0]], axis=0)
    value = jnp.concatenate([v0[0], v1[0], v2[0], v3[0]], axis=0)
    key_t = key.T
    value_t = value.T
    dk = jnp.zeros((4 * seg, DH), jnp.float32)
    dv = jnp.zeros((4 * seg, DH), jnp.float32)
    for pair in range(groups // 2):
        one, two = slice(2 * pair * DH, (2 * pair + 1) * DH), slice((2 * pair + 1) * DH, (2 * pair + 2) * DH)
        q = jnp.concatenate([q_ref[:, one], q_ref[:, two]], axis=0)
        g = jnp.concatenate([g_ref[:, one], g_ref[:, two]], axis=0)
        s = nt(key, q) * fold + bias[...]
        e = jnp.exp2(s - jnp.max(s, axis=0, keepdims=True))
        p = e * (1.0 / jnp.sum(e, axis=0, keepdims=True))
        p_low = p.astype(jnp.bfloat16)
        dp = nt(value, g)
        delta = jnp.sum(p * dp, axis=0, keepdims=True)
        ds = (p * (dp - delta)).astype(jnp.bfloat16)
        o = nn(value_t, p_low).T.astype(jnp.bfloat16)
        o_ref[:, one] = o[:seg]
        o_ref[:, two] = o[seg:]
        dq = (nn(key_t, ds) * scale).T.astype(jnp.bfloat16)
        dq_ref[:, one] = dq[:seg]
        dq_ref[:, two] = dq[seg:]
        dk = dk + nn(ds, q)
        dv = dv + nn(p_low, g)
    dk_ref[...] = (dk * scale).reshape(dk_ref.shape).astype(jnp.bfloat16)
    dv_ref[...] = dv.reshape(dv_ref.shape).astype(jnp.bfloat16)


def attention_call(par, own, q, g, key_all, value_all):
    seg = q.shape[0]
    wide = q.shape[1] // HK

    def slot(i):
        def index(h, par, own):
            return (jnp.maximum(ancestors_of(par, own[0])[i], 0), 0, h)
        return pl.BlockSpec((1, seg, DH), index)

    mine = pl.BlockSpec((1, seg, DH), lambda h, par, own: (own[0], 0, h))
    kv = [slot(0), slot(1), slot(2), mine]
    rows = pl.BlockSpec((seg, wide), lambda h, par, own: (0, h))
    terms = pl.BlockSpec((4, seg, DH), lambda h, par, own: (0, 0, h))
    term = jax.ShapeDtypeStruct((4, seg, HK * DH), jnp.bfloat16)
    return pl.pallas_call(
        attention_kernel,
        out_shape=[jax.ShapeDtypeStruct(q.shape, q.dtype)] * 2 + [term] * 2,
        grid_spec=pltpu.PrefetchScalarGridSpec(
            num_scalar_prefetch=2,
            grid=(HK,),
            in_specs=[rows, rows] + kv + kv,
            out_specs=[rows, rows, terms, terms],
            scratch_shapes=[pltpu.VMEM((4 * seg, 2 * seg), jnp.float32)],
        ),
        compiler_params=pltpu.CompilerParams(vmem_limit_bytes=VMEM_LIMIT),
        cost_estimate=pl.CostEstimate(
            flops=12 * HQ * seg * 4 * seg * DH, bytes_accessed=7000000, transcendentals=HQ * seg * 4 * seg
        ),
    )(par, own, q, g, *([key_all] * 4), *([value_all] * 4))


def reduce_kernel(
    n_leaf, n_grp,
    par, dk_ref, dv_ref, hidden_t, w_ref,
    dkey, dhidden, dweight,
    vx_out, kx_out, vx_in, kx_in, vz_out, kz_out, vz_in, kz_in, hid_all, dv_all,
    part, px_out, px_in, pz_out, pz_in,
    vx_send, vx_recv, kx_send, kx_recv, vz_send, vz_recv, kz_send, kz_recv,
    h_send, h_recv, g_send, g_recv, px_send, px_recv, pz_send, pz_recv,
):
    leaf, grp, z, x, y, c = place()
    nz = n_leaf // NX
    x_peer, y_peer, c_peer = z * NX + (1 - x), (1 - y) * NC + c, y * NC + (1 - c)
    f32, bf16 = jnp.float32, jnp.bfloat16
    chain = ancestors_of(par, leaf)

    def term(ref, target):
        slot = jnp.where(chain[0] == target, 0, jnp.where(chain[1] == target, 1, 2))
        hit = (chain[0] == target) | (chain[1] == target) | (chain[2] == target)
        block = ref[slot]
        return jnp.where(hit, block, jnp.zeros_like(block))

    greet(leaf, grp, n_leaf, n_grp)

    def x_copy(out, into, sems, t):
        return remote(out.at[t], into.at[t], sems[0].at[t], sems[1].at[t], x_peer, grp)

    v_sems, k_sems = (vx_send, vx_recv), (kx_send, kx_recv)
    for ref, out, into, sems in ((dv_ref, vx_out, vx_in, v_sems), (dk_ref, kx_out, kx_in, k_sems)):
        for t in range(nz):
            @pl.when((t < z) | ((t == z) & (x == 1)))
            def _(t=t, ref=ref, out=out, into=into, sems=sems):
                out[t] = term(ref, t * NX + (1 - x))
                x_copy(out, into, sems, t).start()

    hidden = []
    for d in range(1, n_grp):
        to = lax.rem(grp + d, n_grp)
        copy = remote(hidden_t.at[:, to], hid_all.at[d], h_send.at[d - 1], h_recv.at[d - 1], leaf, to)
        copy.start()
        hidden.append(copy)

    def z_copy(out, into, sems, t):
        return remote(out.at[t], into.at[z], sems[0].at[t], sems[1].at[z], t * NX + x, grp)

    vz_sems, kz_sems = (vz_send, vz_recv), (kz_send, kz_recv)
    for ref, out, into, sems, z_out, z_in, z_sems in (
        (dv_ref, vx_out, vx_in, v_sems, vz_out, vz_in, vz_sems),
        (dk_ref, kx_out, kx_in, k_sems, kz_out, kz_in, kz_sems),
    ):
        for t in range(nz - 1):
            @pl.when(t < z)
            def _(t=t, ref=ref, out=out, into=into, sems=sems, z_out=z_out, z_in=z_in, z_sems=z_sems):
                x_copy(out, into, sems, t).wait_recv()
                total = term(ref, t * NX + x).astype(f32) + into[t].astype(f32)
                z_out[t] = total.astype(bf16)
                z_copy(z_out, z_in, z_sems, t).start()

    def owned(ref, out, into, sems, z_in, z_sems, store):
        store(ref[3].astype(f32))

        @pl.when(x == 0)
        def _():
            for t in range(nz):
                @pl.when(t == z)
                def _(t=t):
                    x_copy(out, into, sems, t).wait_recv()
                    store(into[t].astype(f32), True)

        for t in range(1, nz):
            @pl.when(t > z)
            def _(t=t):
                remote(z_in.at[t], z_in.at[t], z_sems[0].at[t - 1], z_sems[1].at[t], t * NX + x, grp).wait_recv()
                store(z_in[t].astype(f32), True)

    acc = part.at[0]

    def keep(value, more=False):
        acc[...] = acc[...] + value if more else value

    owned(dv_ref, vx_out, vx_in, v_sems, vz_in, vz_sems, keep)
    dv_low = acc[...].astype(bf16)
    dv_all[grp] = dv_low
    mine = dv_all.at[grp]
    to_y = remote(mine, mine, g_send.at[0], g_recv.at[0], leaf, y_peer)
    to_c = remote(mine, mine, g_send.at[1], g_recv.at[1], leaf, c_peer)
    to_y.start()
    to_c.start()

    width = w_ref.shape[0] // 4
    for i in range(2):
        dhidden[:, i * width : (i + 1) * width] = nt(dv_low, w_ref[i * width : (i + 1) * width, :]).astype(bf16)

    to_y.wait_recv()
    theirs = dv_all.at[y_peer]
    relay = remote(theirs, theirs, g_send.at[2], g_recv.at[2], leaf, c_peer)
    relay.start()
    for i in range(2, 4):
        dhidden[:, i * width : (i + 1) * width] = nt(dv_low, w_ref[i * width : (i + 1) * width, :]).astype(bf16)
    for copy in hidden:
        copy.wait_recv()
    to_c.wait_recv()
    relay.wait_recv()

    def partial_at(target):
        total = nn(hidden_t[target, grp], dv_all[grp])
        for d in range(1, n_grp):
            total = total + nn(hid_all[d, target], dv_all[lax.rem(grp + n_grp - d, n_grp)])
        return total

    px = []
    for t in range(nz):
        px_out[t] = partial_at(t * NX + (1 - x)).astype(bf16)
        copy = remote(px_out.at[t], px_in.at[t], px_send.at[t], px_recv.at[t], x_peer, grp)
        copy.start()
        px.append(copy)
    pz = []
    for d in range(1, nz):
        t = lax.rem(z + d, nz)
        pz_out[d - 1] = partial_at(t * NX + x).astype(bf16)
    dweight[...] = partial_at(leaf)
    for copy in px:
        copy.wait_recv()
    for d in range(1, nz):
        t = lax.rem(z + d, nz)
        pz_out[d - 1] = (pz_out[d - 1].astype(f32) + px_in[t].astype(f32)).astype(bf16)
        copy = remote(pz_out.at[d - 1], pz_in.at[d - 1], pz_send.at[d - 1], pz_recv.at[d - 1], t * NX + x, grp)
        copy.start()
        pz.append(copy)
    dweight[...] += px_in[z].astype(f32)

    owned(dk_ref, kx_out, kx_in, k_sems, kz_in, kz_sems, keep)
    dkey[...] = acc[...].astype(bf16)

    for copy in pz:
        copy.wait_recv()
    for d in range(1, nz):
        dweight[...] += pz_in[d - 1].astype(f32)

    for out, into, sems in ((vx_out, vx_in, v_sems), (kx_out, kx_in, k_sems)):
        for t in range(nz):
            @pl.when((t < z) | ((t == z) & (x == 1)))
            def _(t=t, out=out, into=into, sems=sems):
                x_copy(out, into, sems, t).wait_send()
    for out, into, sems in ((vz_out, vz_in, vz_sems), (kz_out, kz_in, kz_sems)):
        for t in range(nz - 1):
            @pl.when(t < z)
            def _(t=t, out=out, into=into, sems=sems):
                z_copy(out, into, sems, t).wait_send()
    for copy in hidden + [to_y, to_c, relay] + px + pz:
        copy.wait_send()


def reduce_call(par, dk, dv, hidden_t, w, n_leaf, n_grp):
    nz = n_leaf // NX
    _, seg, width = dk.shape
    rows = hidden_t.shape[2]
    bf16 = jnp.bfloat16
    vmem = pl.BlockSpec(memory_space=pltpu.VMEM)
    dma = pltpu.SemaphoreType.DMA
    block = lambda n: pltpu.VMEM((n, seg, width), bf16)
    piece = lambda n: pltpu.VMEM((n, rows, width), bf16)
    return pl.pallas_call(
        functools.partial(reduce_kernel, n_leaf, n_grp),
        out_shape=[
            jax.ShapeDtypeStruct((seg, width), bf16),
            jax.ShapeDtypeStruct((seg, w.shape[0]), bf16),
            jax.ShapeDtypeStruct((rows, width), jnp.float32),
        ],
        in_specs=[pl.BlockSpec(memory_space=pltpu.SMEM)] + [vmem] * 4,
        out_specs=[vmem] * 3,
        scratch_shapes=[block(nz)] * 8
        + [
            pltpu.VMEM((n_grp, n_leaf, rows, seg), bf16),
            block(n_grp),
            pltpu.VMEM((1, seg, width), jnp.float32),
            piece(nz), piece(nz), piece(nz - 1), piece(nz - 1),
        ]
        + [dma((nz,))] * 8
        + [dma((n_grp - 1,))] * 2
        + [dma((3,))] * 2
        + [dma((nz,))] * 2
        + [dma((nz - 1,))] * 2,
        compiler_params=pltpu.CompilerParams(
            collective_id=1, has_side_effects=True, vmem_limit_bytes=VMEM_LIMIT
        ),
        cost_estimate=pl.CostEstimate(flops=4 * 128 * 2560 * 512, bytes_accessed=8000000, transcendentals=0),
    )(par, dk, dv, hidden_t, w)


def fast_shards(n_leaf, n_grp, hidden_states, query_rows, key_rows, value_weight, parent_links, out_grad):
    hidden = hidden_states[0]
    own = lax.axis_index("leaf").astype(jnp.int32).reshape(1)
    w_all, key_all, value_all, parents = gather_call(
        parent_links, value_weight, key_rows[0], hidden, n_leaf, n_grp
    )
    par = parents[:, 0, 0]
    rows, width = value_weight.shape
    w = w_all.reshape(hidden.shape[1], width)
    hidden_t = hidden.T.reshape(n_leaf, n_grp, rows, hidden.shape[0])
    out, dq, dk, dv = attention_call(par, own, query_rows[0], out_grad[0], key_all, value_all)
    dkey, dhidden, dweight = reduce_call(par, dk, dv, hidden_t, w, n_leaf, n_grp)
    return out[None], dq[None], dkey[None], dhidden[None], dweight


def chain_slots(parent_list, own_index):
    total = parent_list.shape[0]

    def parent_of(node_index):
        hit = jnp.arange(total, dtype=jnp.int32) == node_index
        found = jnp.sum(jnp.where(hit, parent_list, 0))
        return jnp.where(node_index >= 0, found, -1)

    first = parent_of(own_index)
    second = parent_of(first)
    third = parent_of(second)
    return jnp.stack([first, second, third])


def key_mask(ancestors, segment_len):
    valid = jnp.concatenate([ancestors >= 0, jnp.ones((1,), bool)])
    block_ok = jnp.repeat(valid, segment_len)[None, :]
    row_ids = jnp.arange(segment_len, dtype=jnp.int32)[:, None]
    col_ids = jnp.arange(4 * segment_len, dtype=jnp.int32)[None, :]
    causal = (col_ids < 3 * segment_len) | (col_ids - 3 * segment_len <= row_ids)
    return block_ok & causal


def segment_pass(query_seg, key_all, value_all, grad_seg, visible):
    segment_len = query_seg.shape[0]
    groups = HQ // HK
    scale_factor = 1.0 / DH**0.5
    query_heads = query_seg.reshape(segment_len, HK, groups, DH)
    key_heads = key_all.reshape(-1, HK, DH)
    value_heads = value_all.reshape(-1, HK, DH)
    grad_heads = grad_seg.reshape(segment_len, HK, groups, DH)
    scores = (
        jnp.einsum("rhgd,khd->hgrk", query_heads, key_heads, preferred_element_type=jnp.float32)
        * scale_factor
    )
    scores = jnp.where(visible, scores, -1e30)
    row_max = jnp.max(scores, axis=-1, keepdims=True)
    weights_exp = jnp.where(visible, jnp.exp(scores - row_max), 0.0)
    probs = weights_exp / jnp.sum(weights_exp, axis=-1, keepdims=True)
    probs_low = probs.astype(jnp.bfloat16)
    output = jnp.einsum(
        "hgrk,khd->rhgd", probs_low, value_heads, preferred_element_type=jnp.float32
    )
    output = output.reshape(segment_len, HQ * DH).astype(jnp.bfloat16)
    dprobs = jnp.einsum(
        "rhgd,khd->hgrk", grad_heads, value_heads, preferred_element_type=jnp.float32
    )
    delta = jnp.sum(probs * dprobs, axis=-1, keepdims=True)
    dscores = (probs * (dprobs - delta)).astype(jnp.bfloat16)
    query_grad = (
        jnp.einsum("hgrk,khd->rhgd", dscores, key_heads, preferred_element_type=jnp.float32)
        * scale_factor
    )
    query_grad = query_grad.reshape(segment_len, HQ * DH).astype(jnp.bfloat16)
    key_part = (
        jnp.einsum("hgrk,rhgd->khd", dscores, query_heads, preferred_element_type=jnp.float32)
        * scale_factor
    )
    value_part = jnp.einsum(
        "hgrk,rhgd->khd", probs_low, grad_heads, preferred_element_type=jnp.float32
    )
    grad_term = jnp.concatenate(
        [key_part.reshape(-1, HK * DH), value_part.reshape(-1, HK * DH)], axis=1
    )
    return (output, query_grad, grad_term)


def shards(hidden_states, query_rows, key_rows, value_weight, parent_links, out_grad):
    hidden_local = hidden_states[0]
    query_local = query_rows[0]
    key_local = key_rows[0]
    grad_local = out_grad[0]
    segment_len = hidden_local.shape[0]
    key_width = key_local.shape[1]
    parent_list = lax.all_gather(parent_links, "leaf", axis=1, tiled=True)[0]
    own_index = lax.axis_index("leaf")
    ancestors = chain_slots(parent_list, own_index)
    columns = hidden_local
    values = jnp.dot(
        columns,
        lax.all_gather(value_weight, ("leaf", "grp"), axis=0, tiled=True),
        preferred_element_type=jnp.float32,
    )
    values = values.astype(jnp.bfloat16)
    key_value = jnp.concatenate([key_local, values], axis=1)
    every_segment = lax.all_gather(key_value, "leaf", axis=0, tiled=True)
    fetched = jnp.concatenate(
        [
            lax.dynamic_slice_in_dim(
                every_segment, jnp.maximum(ancestors[i], 0) * segment_len, segment_len, 0
            )
            for i in range(3)
        ],
        axis=0,
    )
    gathered = jnp.concatenate([fetched, key_value], axis=0)
    output, query_grad, grad_term = segment_pass(
        query_local,
        gathered[:, :key_width],
        gathered[:, key_width:],
        grad_local,
        key_mask(ancestors, segment_len),
    )
    grad_low = grad_term.astype(jnp.bfloat16)
    owners = jnp.concatenate([ancestors, own_index[None]])
    grad_wide = grad_low.astype(jnp.float32)
    targets = (
        owners[:, None] * segment_len + jnp.arange(segment_len, dtype=jnp.int32)[None, :]
    ).reshape(-1)
    keep_rows = (
        jnp.repeat(owners >= 0, segment_len)
        & (targets >= 0)
        & (targets < segment_len * lax.axis_size("leaf"))
    )
    targets = jnp.where(keep_rows, targets, segment_len * lax.axis_size("leaf"))
    sums = lax.psum_scatter(
        jnp.zeros((segment_len * lax.axis_size("leaf"), grad_wide.shape[1]), grad_wide.dtype)
        .at[targets]
        .add(grad_wide, mode="drop")
        .astype(jnp.bfloat16),
        "leaf",
        scatter_dimension=0,
        tiled=True,
    ).astype(jnp.float32)
    key_grad = sums[:, :key_width].astype(jnp.bfloat16)
    value_grad = sums[:, key_width:].astype(jnp.bfloat16)
    columns = hidden_local
    weight_grad = lax.psum_scatter(
        lax.dot_general(
            columns, value_grad, (((0,), (0,)), ((), ())), preferred_element_type=jnp.float32
        ),
        ("leaf", "grp"),
        scatter_dimension=0,
        tiled=True,
    )
    hidden_grad = lax.dot_general(
        value_grad,
        lax.all_gather(value_weight, ("leaf", "grp"), axis=0, tiled=True),
        (((1,), (1,)), ((), ())),
        preferred_element_type=jnp.float32,
    )
    hidden_grad = hidden_grad.astype(jnp.bfloat16)
    return (output[None], query_grad[None], key_grad[None], hidden_grad[None], weight_grad)


def solution(mesh):
    placed = (
        P("grp", "leaf", None),
        P("grp", "leaf", None),
        P("grp", "leaf", None),
        P(("leaf", "grp"), None),
        P("grp", "leaf"),
        P("grp", "leaf", None),
    )
    n_leaf, n_grp = mesh.shape["leaf"], mesh.shape["grp"]

    def body(hidden_states, query_rows, key_rows, value_weight, parent_links, out_grad):
        args = (hidden_states, query_rows, key_rows, value_weight, parent_links, out_grad)
        if n_leaf % NX == 0 and n_grp == 2 * NC and value_weight.shape[0] % 16 == 0:
            return fast_shards(n_leaf, n_grp, *args)
        return shards(*args)

    return jax.shard_map(
        body,
        mesh=mesh,
        in_specs=placed,
        out_specs=(
            P("grp", "leaf", None),
            P("grp", "leaf", None),
            P("grp", "leaf", None),
            P("grp", "leaf", None),
            P(("leaf", "grp"), None),
        ),
        check_vma=False,
    )
```

```python
import functools

import jax
import jax.numpy as jnp
from jax import lax
from jax.experimental import pallas as pl
from jax.experimental.pallas import tpu as pltpu
from jax.sharding import PartitionSpec as P

HQ = 40
HK = 4
DH = 128
MESH = pl.DeviceIdType.MESH
NX = 2
NC = 2
VMEM_LIMIT = 56 * 1024 * 1024


def nt(a, b):
    return lax.dot_general(a, b, (((1,), (1,)), ((), ())), preferred_element_type=jnp.float32)


def nn(a, b):
    return jnp.dot(a, b, preferred_element_type=jnp.float32)


def place():
    leaf = lax.axis_index("leaf")
    grp = lax.axis_index("grp")
    return leaf, grp, leaf // NX, leaf % NX, grp // NC, grp % NC


def remote(src, dst, send, recv, leaf, grp):
    return pltpu.make_async_remote_copy(
        src_ref=src,
        dst_ref=dst,
        send_sem=send,
        recv_sem=recv,
        device_id=(leaf, grp),
        device_id_type=MESH,
    )


def greet(leaf, grp, n_leaf, n_grp):
    barrier = pltpu.get_barrier_semaphore()
    for step in range(1, n_leaf):
        pl.semaphore_signal(
            barrier, inc=1, device_id=(lax.rem(leaf + step, n_leaf), grp), device_id_type=MESH
        )
    for step in range(1, n_grp):
        pl.semaphore_signal(
            barrier, inc=1, device_id=(leaf, lax.rem(grp + step, n_grp)), device_id_type=MESH
        )
    pl.semaphore_wait(barrier, n_leaf + n_grp - 2)


def ancestors_of(par, own):
    first = par[own, 0]
    second = jnp.where(first >= 0, par[jnp.maximum(first, 0), 0], -1)
    third = jnp.where(second >= 0, par[jnp.maximum(second, 0), 0], -1)
    return first, second, third


def tree_kernel(
    n_leaf, n_grp,
    parent_ref, w_ref, key_ref, hidden_ref, hidden_t, q_hbm, g_hbm,
    out_ref, dq_ref, dkey, dhidden, dweight,
    q_ref, g_ref, w_all, key_all, v0, v1, v2, v3, parents, own_parent, par, bias, terms,
    x_out, x_in, z_out, z_in, acc, hid_all, dv_all, px_out, px_in, pz_out, pz_in,
    load_sem, par_send, par_recv, wz_send, wz_recv, w_send, w_recv, c_send, c_recv,
    kz_send, kz_recv, kx_send, kx_recv, vz_send, vz_recv, vx_send, vx_recv,
    gx_send, gx_recv, gz_send, gz_recv, h_send, h_recv, d_send, d_recv,
    px_send, px_recv, pz_send, pz_recv,
):
    leaf, grp, z, x, y, c = place()
    nz = n_leaf // NX
    seg = key_ref.shape[0]
    f32, bf16 = jnp.float32, jnp.bfloat16
    scale = 1.0 / DH**0.5
    fold = scale * 1.4426950408889634
    x_peer, y_peer, c_peer = z * NX + (1 - x), (1 - y) * NC + c, y * NC + (1 - c)
    values = (v0, v1, v2, v3)
    half = w_ref.shape[1] // 2
    low, high = pl.ds(0, half), pl.ds(half, half)
    pending = []

    loads = [
        pltpu.make_async_copy(q_hbm, q_ref, load_sem.at[0]),
        pltpu.make_async_copy(g_hbm, g_ref, load_sem.at[1]),
    ]
    for load in loads:
        load.start()
    own_parent[...] = jnp.full(own_parent.shape, parent_ref[0, 0], jnp.int32)
    greet(leaf, grp, n_leaf, n_grp)

    def start(copy):
        copy.start()
        pending.append(copy)
        return copy

    wz = []
    for d in range(1, nz):
        to = lax.rem(z + d, nz)
        wz.append(
            start(remote(w_ref, w_all.at[z, x, y, c], wz_send.at[d - 1], wz_recv.at[d - 1], to * NX + x, grp))
        )
    links = []
    for d in range(1, n_leaf):
        to = lax.rem(leaf + d, n_leaf)
        links.append(
            start(remote(own_parent, parents.at[leaf], par_send.at[d - 1], par_recv.at[d - 1], to, grp))
        )
    w_all[z, x, y, c] = w_ref[...]
    key_all[leaf] = key_ref[...]
    parents[leaf] = own_parent[...]

    def up_copy(block, whole, sems, d):
        return remote(block, whole.at[leaf], sems[0].at[d - 1], sems[1].at[d - 1], leaf + d * NX, grp)

    def up_start(block, whole, sems):
        for d in range(1, nz):
            @pl.when(z + d < nz)
            def _(d=d):
                up_copy(block, whole, sems, d).start()

    def across_own(block, whole, sems):
        @pl.when(x == 0)
        def _():
            remote(block, whole.at[leaf], sems[0].at[0], sems[1].at[0], x_peer, grp).start()

    def across_copy(whole, sems, d):
        slot = leaf - d * NX
        return remote(whole.at[slot], whole.at[slot], sems[0].at[d], sems[1].at[d], x_peer, grp)

    def across_start(whole, up_sems, sems):
        for d in range(1, nz):
            @pl.when(z - d >= 0)
            def _(d=d):
                slot = leaf - d * NX
                remote(whole.at[slot], whole.at[slot], up_sems[0].at[d - 1], up_sems[1].at[d - 1], leaf, grp).wait_recv()
                across_copy(whole, sems, d).start()

    def across_ready(block, whole, sems):
        for d in range(1, nz):
            @pl.when(z - d >= 0)
            def _(d=d):
                slot = x_peer - d * NX
                remote(whole.at[slot], whole.at[slot], sems[0].at[d], sems[1].at[d], x_peer, grp).wait_recv()

        @pl.when(x == 1)
        def _():
            remote(block, whole.at[x_peer], sems[0].at[0], sems[1].at[0], x_peer, grp).wait_recv()

    def sent(block, whole, up_sems, sems):
        for d in range(1, nz):
            @pl.when(z + d < nz)
            def _(d=d):
                up_copy(block, whole, up_sems, d).wait_send()

            @pl.when(z - d >= 0)
            def _(d=d):
                across_copy(whole, sems, d).wait_send()

        @pl.when(x == 0)
        def _():
            remote(block, whole.at[leaf], sems[0].at[0], sems[1].at[0], x_peer, grp).wait_send()

    k_up, k_across = (kz_send, kz_recv), (kx_send, kx_recv)

    for copy in wz:
        copy.wait_recv()
    column_a = w_all.at[:, x, y, c, :, low]
    column_b = w_all.at[:, x, y, c, :, high]
    first_a = start(remote(column_a, column_a, w_send.at[0], w_recv.at[0], x_peer, grp))
    first_b = start(remote(column_b, column_b, w_send.at[1], w_recv.at[1], leaf, y_peer))
    whole_c = w_all.at[:, x, y, c]
    to_core = [start(remote(whole_c, whole_c, c_send.at[0], c_recv.at[0], leaf, c_peer))]
    up_start(key_ref, key_all, k_up)

    first_a.wait_recv()
    plane_a = w_all.at[:, :, y, c, :, low]
    second_a = start(remote(plane_a, plane_a, w_send.at[2], w_recv.at[2], leaf, y_peer))
    first_b.wait_recv()
    plane_b = w_all.at[:, x, :, c, :, high]
    second_b = start(remote(plane_b, plane_b, w_send.at[3], w_recv.at[3], x_peer, grp))
    got_a = w_all.at[:, 1 - x, y, c, :, low]
    got_b = w_all.at[:, x, 1 - y, c, :, high]
    to_core.append(start(remote(got_a, got_a, c_send.at[1], c_recv.at[1], leaf, c_peer)))
    to_core.append(start(remote(got_b, got_b, c_send.at[2], c_recv.at[2], leaf, c_peer)))
    second_a.wait_recv()
    late_a = w_all.at[:, :, 1 - y, c, :, low]
    to_core.append(start(remote(late_a, late_a, c_send.at[3], c_recv.at[3], leaf, c_peer)))
    second_b.wait_recv()
    late_b = w_all.at[:, 1 - x, :, c, :, high]
    to_core.append(start(remote(late_b, late_b, c_send.at[4], c_recv.at[4], leaf, c_peer)))

    across_own(key_ref, key_all, k_across)
    across_start(key_all, k_up, k_across)
    hidden = []
    for d in range(1, n_grp):
        to = lax.rem(grp + d, n_grp)
        hidden.append(
            start(remote(hidden_t.at[to], hid_all.at[d], h_send.at[d - 1], h_recv.at[d - 1], leaf, to))
        )
    for copy in to_core:
        copy.wait_recv()

    weight = w_all[...].reshape(hidden_ref.shape[1], w_ref.shape[1])

    def v_sems(h):
        return (vz_send.at[h], vz_recv.at[h]), (vx_send.at[h], vx_recv.at[h])

    for part in range(2):
        pair = nn(hidden_ref[...], weight[:, part * half : (part + 1) * half]).astype(bf16)
        for i in range(HK // 2):
            h = part * (HK // 2) + i
            whole = values[h]
            whole[leaf] = pair[:, i * DH : (i + 1) * DH]
            up, across = v_sems(h)
            up_start(whole.at[leaf], whole, up)
            across_own(whole.at[leaf], whole, across)

    for copy in links:
        copy.wait_recv()
    listing = pltpu.make_async_copy(parents.at[:, 0], par, load_sem.at[2])
    listing.start()

    def forward(h):
        if h < HK:
            up, across = v_sems(h)
            across_start(values[h], up, across)

    forward(0)
    listing.wait()
    chain = ancestors_of(par, leaf)
    for i in range(3):
        bias[i * seg : (i + 1) * seg, :] = jnp.full(
            (seg, 2 * seg), jnp.where(chain[i] >= 0, 0.0, -1e30), f32
        )
    col = lax.broadcasted_iota(jnp.int32, (seg, 2 * seg), 0)
    row = lax.broadcasted_iota(jnp.int32, (seg, 2 * seg), 1)
    row = jnp.where(row >= seg, row - seg, row)
    bias[3 * seg :, :] = jnp.where(col <= row, 0.0, -1e30)
    across_ready(key_ref, key_all, k_across)
    for load in loads:
        load.wait()
    forward(1)

    def head(h, hook):
        up, across = v_sems(h)
        across_ready(values[h].at[leaf], values[h], across)
        lanes = slice(h * DH, (h + 1) * DH)
        slots = [jnp.maximum(chain[i], 0) for i in range(3)] + [leaf]
        key = jnp.concatenate([key_all[slot, :, lanes] for slot in slots], axis=0)
        value = jnp.concatenate([values[h][slot] for slot in slots], axis=0)
        key_t = key.T
        value_t = value.T
        dk = jnp.zeros((4 * seg, DH), f32)
        dv = jnp.zeros((4 * seg, DH), f32)
        groups = HQ // HK
        for pair in range(groups // 2):
            at = (h * groups + 2 * pair) * DH
            one, two = slice(at, at + DH), slice(at + DH, at + 2 * DH)
            q = jnp.concatenate([q_ref[:, one], q_ref[:, two]], axis=0)
            g = jnp.concatenate([g_ref[:, one], g_ref[:, two]], axis=0)
            s = nt(key, q) * fold + bias[...]
            e = jnp.exp2(s - jnp.max(s, axis=0, keepdims=True))
            p = e * (1.0 / jnp.sum(e, axis=0, keepdims=True))
            p_low = p.astype(bf16)
            dp = nt(value, g)
            delta = jnp.sum(p * dp, axis=0, keepdims=True)
            ds = (p * (dp - delta)).astype(bf16)
            o = nn(value_t, p_low).T.astype(bf16)
            out_ref[:, one] = o[:seg]
            out_ref[:, two] = o[seg:]
            dq = (nn(key_t, ds) * scale).T.astype(bf16)
            dq_ref[:, one] = dq[:seg]
            dq_ref[:, two] = dq[seg:]
            dk = dk + nn(ds, q)
            dv = dv + nn(p_low, g)
            if pair == 1:
                hook()
        for i in range(4):
            terms[h, i, :, :DH] = (dk[i * seg : (i + 1) * seg] * scale).astype(bf16)
            terms[h, i, :, DH:] = dv[i * seg : (i + 1) * seg].astype(bf16)

    def term(h, target):
        slot = jnp.where(chain[0] == target, 0, jnp.where(chain[1] == target, 1, 2))
        hit = (chain[0] == target) | (chain[1] == target) | (chain[2] == target)
        block = terms[h, slot]
        return jnp.where(hit, block, jnp.zeros_like(block))

    def x_copy(h, t):
        return remote(x_out.at[h, t], x_in.at[h, t], gx_send.at[h, t], gx_recv.at[h, t], x_peer, grp)

    def z_copy(h, t):
        return remote(z_out.at[h, t], z_in.at[h, z], gz_send.at[h, t], gz_recv.at[h, z], t * NX + x, grp)

    def x_stage(h):
        for t in range(nz):
            @pl.when((t < z) | ((t == z) & (x == 1)))
            def _(t=t):
                x_out[h, t] = term(h, t * NX + (1 - x))
                x_copy(h, t).start()

    def z_stage(h):
        for t in range(nz - 1):
            @pl.when(t < z)
            def _(t=t):
                x_copy(h, t).wait_recv()
                total = term(h, t * NX + x).astype(f32) + x_in[h, t].astype(f32)
                z_out[h, t] = total.astype(bf16)
                z_copy(h, t).start()

    def owned(h):
        acc[...] = terms[h, 3].astype(f32)
        for t in range(nz):
            @pl.when((t == z) & (x == 0))
            def _(t=t):
                x_copy(h, t).wait_recv()
                acc[...] += x_in[h, t].astype(f32)

        for t in range(1, nz):
            @pl.when(t > z)
            def _(t=t):
                block = z_in.at[h, t]
                remote(block, block, gz_send.at[h, t], gz_recv.at[h, t], t * NX + x, grp).wait_recv()
                acc[...] += z_in[h, t].astype(f32)

        lanes = slice(h * DH, (h + 1) * DH)
        dkey[:, lanes] = acc[:, :DH].astype(bf16)
        dv_all[h // 2, grp, :, (h % 2) * DH : (h % 2 + 1) * DH] = acc[:, DH:].astype(bf16)

    def spread(part):
        mine = dv_all.at[part, grp]
        to_y = start(remote(mine, mine, d_send.at[part, 0], d_recv.at[part, 0], leaf, y_peer))
        to_c = start(remote(mine, mine, d_send.at[part, 1], d_recv.at[part, 1], leaf, c_peer))
        return to_y, to_c

    def relay(part, to_y):
        to_y.wait_recv()
        theirs = dv_all.at[part, y_peer]
        return start(remote(theirs, theirs, d_send.at[part, 2], d_recv.at[part, 2], leaf, c_peer))

    rows = hidden_t.shape[3]

    def partials(part, side):
        total = nn(hidden_t[grp, side].reshape(nz * rows, seg), dv_all[part, grp])
        for d in range(1, n_grp):
            owner = lax.rem(grp + n_grp - d, n_grp)
            total = total + nn(hid_all[d, side].reshape(nz * rows, seg), dv_all[part, owner])
        return total

    def px_copy(part):
        return remote(px_out.at[part], px_in.at[part], px_send.at[part], px_recv.at[part], x_peer, grp)

    def weight_x(part):
        total = partials(part, 1 - x).astype(bf16)
        px_out[part] = total.reshape(nz, rows, half)
        start(px_copy(part))
        pz_out[part] = partials(part, x).reshape(nz, rows, half)

    def weight_z(part):
        px_copy(part).wait_recv()
        copies = []
        for d in range(1, nz):
            t = lax.rem(z + d, nz)
            px_out_z = pz_out[part, t] + px_in[part, t].astype(f32)
            pz_in[part, 0, d - 1] = px_out_z.astype(bf16)
            copies.append(
                start(
                    remote(
                        pz_in.at[part, 0, d - 1], pz_in.at[part, 1, d - 1],
                        pz_send.at[part, d - 1], pz_recv.at[part, d - 1], t * NX + x, grp,
                    )
                )
            )
        return copies

    head(0, lambda: forward(2))
    x_stage(0)
    head(1, lambda: forward(3))
    x_stage(1)
    z_stage(0)
    head(2, lambda: None)
    x_stage(2)
    z_stage(1)
    head(3, lambda: None)
    x_stage(3)
    z_stage(2)
    owned(0)
    owned(1)
    to_y, to_c = spread(0)
    for copy in hidden:
        copy.wait_recv()
    z_stage(3)
    relayed = relay(0, to_y)
    to_c.wait_recv()
    relayed.wait_recv()
    weight_x(0)
    owned(2)
    owned(3)
    to_y, to_c = spread(1)
    width = hidden_ref.shape[1] // 4
    weight = w_all[...].reshape(hidden_ref.shape[1], w_ref.shape[1])
    dv_low = jnp.concatenate([dv_all[0, grp], dv_all[1, grp]], axis=1)
    copies = weight_z(0)
    relayed = relay(1, to_y)
    to_c.wait_recv()
    relayed.wait_recv()
    weight_x(1)
    for i in range(4):
        dhidden[:, i * width : (i + 1) * width] = nt(dv_low, weight[i * width : (i + 1) * width, :]).astype(bf16)
    copies += weight_z(1)
    for copy in copies:
        copy.wait_recv()
    for part in range(2):
        total = pz_out[part, z] + px_in[part, z].astype(f32)
        for d in range(1, nz):
            total = total + pz_in[part, 1, d - 1].astype(f32)
        dweight[:, part * half : (part + 1) * half] = total

    sent(key_ref, key_all, k_up, k_across)
    for h in range(HK):
        up, across = v_sems(h)
        sent(values[h].at[leaf], values[h], up, across)
        for t in range(nz):
            @pl.when((t < z) | ((t == z) & (x == 1)))
            def _(t=t, h=h):
                x_copy(h, t).wait_send()
        for t in range(nz - 1):
            @pl.when(t < z)
            def _(t=t, h=h):
                z_copy(h, t).wait_send()
    for copy in pending:
        copy.wait_send()


def fast_shards(n_leaf, n_grp, hidden_states, query_rows, key_rows, value_weight, parent_links, out_grad):
    hidden, q, g, key = hidden_states[0], query_rows[0], out_grad[0], key_rows[0]
    rows, width = value_weight.shape
    seg, features = hidden.shape
    nz, ny = n_leaf // NX, n_grp // NC
    half = width // 2
    bf16, f32 = jnp.bfloat16, jnp.float32
    hidden_t = hidden.T.reshape(nz, NX, n_grp, rows, seg).transpose(2, 1, 0, 3, 4)
    vmem = pl.BlockSpec(memory_space=pltpu.VMEM)
    anywhere = pl.BlockSpec(memory_space=pl.ANY)
    held, dma = pltpu.VMEM, pltpu.SemaphoreType.DMA
    pairs = lambda *dims: [dma(dims)] * 2
    out, dq, dkey, dhidden, dweight = pl.pallas_call(
        functools.partial(tree_kernel, n_leaf, n_grp),
        out_shape=[
            jax.ShapeDtypeStruct(q.shape, bf16),
            jax.ShapeDtypeStruct(q.shape, bf16),
            jax.ShapeDtypeStruct(key.shape, bf16),
            jax.ShapeDtypeStruct(hidden.shape, bf16),
            jax.ShapeDtypeStruct(value_weight.shape, f32),
        ],
        in_specs=[pl.BlockSpec(memory_space=pltpu.SMEM)] + [vmem] * 4 + [anywhere] * 2,
        out_specs=[vmem] * 5,
        scratch_shapes=[
            held(q.shape, bf16),
            held(q.shape, bf16),
            held((nz, NX, ny, NC, rows, width), bf16),
            held((n_leaf, seg, width), bf16),
        ]
        + [held((n_leaf, seg, DH), bf16)] * HK
        + [
            held((n_leaf, 8, 128), jnp.int32),
            held((8, 128), jnp.int32),
            pltpu.SMEM((n_leaf, 128), jnp.int32),
            held((4 * seg, 2 * seg), f32),
            held((HK, 4, seg, 2 * DH), bf16),
        ]
        + [held((HK, nz, seg, 2 * DH), bf16)] * 4
        + [
            held((seg, 2 * DH), f32),
            held((n_grp, NX, nz, rows, seg), bf16),
            held((2, n_grp, seg, half), bf16),
            held((2, nz, rows, half), bf16),
            held((2, nz, rows, half), bf16),
            held((2, nz, rows, half), f32),
            held((2, 2, nz - 1, rows, half), bf16),
            dma((3,)),
        ]
        + pairs(n_leaf - 1)
        + pairs(nz - 1)
        + pairs(4)
        + pairs(5)
        + pairs(nz - 1)
        + pairs(nz)
        + pairs(HK, nz - 1)
        + pairs(HK, nz)
        + pairs(HK, nz) * 2
        + pairs(n_grp - 1)
        + pairs(2, 3)
        + pairs(2)
        + pairs(2, nz - 1),
        compiler_params=pltpu.CompilerParams(
            collective_id=0, has_side_effects=True, vmem_limit_bytes=VMEM_LIMIT
        ),
        cost_estimate=pl.CostEstimate(
            flops=12 * HQ * seg * 4 * seg * DH + 6 * seg * features * width,
            bytes_accessed=10000000,
            transcendentals=HQ * seg * 4 * seg,
        ),
    )(parent_links, value_weight, key, hidden, hidden_t, q, g)
    return out[None], dq[None], dkey[None], dhidden[None], dweight


def chain_slots(parent_list, own_index):
    total = parent_list.shape[0]

    def parent_of(node_index):
        hit = jnp.arange(total, dtype=jnp.int32) == node_index
        found = jnp.sum(jnp.where(hit, parent_list, 0))
        return jnp.where(node_index >= 0, found, -1)

    first = parent_of(own_index)
    second = parent_of(first)
    third = parent_of(second)
    return jnp.stack([first, second, third])


def key_mask(ancestors, segment_len):
    valid = jnp.concatenate([ancestors >= 0, jnp.ones((1,), bool)])
    block_ok = jnp.repeat(valid, segment_len)[None, :]
    row_ids = jnp.arange(segment_len, dtype=jnp.int32)[:, None]
    col_ids = jnp.arange(4 * segment_len, dtype=jnp.int32)[None, :]
    causal = (col_ids < 3 * segment_len) | (col_ids - 3 * segment_len <= row_ids)
    return block_ok & causal


def segment_pass(query_seg, key_all, value_all, grad_seg, visible):
    segment_len = query_seg.shape[0]
    groups = HQ // HK
    scale_factor = 1.0 / DH**0.5
    query_heads = query_seg.reshape(segment_len, HK, groups, DH)
    key_heads = key_all.reshape(-1, HK, DH)
    value_heads = value_all.reshape(-1, HK, DH)
    grad_heads = grad_seg.reshape(segment_len, HK, groups, DH)
    scores = (
        jnp.einsum("rhgd,khd->hgrk", query_heads, key_heads, preferred_element_type=jnp.float32)
        * scale_factor
    )
    scores = jnp.where(visible, scores, -1e30)
    row_max = jnp.max(scores, axis=-1, keepdims=True)
    weights_exp = jnp.where(visible, jnp.exp(scores - row_max), 0.0)
    probs = weights_exp / jnp.sum(weights_exp, axis=-1, keepdims=True)
    probs_low = probs.astype(jnp.bfloat16)
    output = jnp.einsum(
        "hgrk,khd->rhgd", probs_low, value_heads, preferred_element_type=jnp.float32
    )
    output = output.reshape(segment_len, HQ * DH).astype(jnp.bfloat16)
    dprobs = jnp.einsum(
        "rhgd,khd->hgrk", grad_heads, value_heads, preferred_element_type=jnp.float32
    )
    delta = jnp.sum(probs * dprobs, axis=-1, keepdims=True)
    dscores = (probs * (dprobs - delta)).astype(jnp.bfloat16)
    query_grad = (
        jnp.einsum("hgrk,khd->rhgd", dscores, key_heads, preferred_element_type=jnp.float32)
        * scale_factor
    )
    query_grad = query_grad.reshape(segment_len, HQ * DH).astype(jnp.bfloat16)
    key_part = (
        jnp.einsum("hgrk,rhgd->khd", dscores, query_heads, preferred_element_type=jnp.float32)
        * scale_factor
    )
    value_part = jnp.einsum(
        "hgrk,rhgd->khd", probs_low, grad_heads, preferred_element_type=jnp.float32
    )
    grad_term = jnp.concatenate(
        [key_part.reshape(-1, HK * DH), value_part.reshape(-1, HK * DH)], axis=1
    )
    return (output, query_grad, grad_term)


def shards(hidden_states, query_rows, key_rows, value_weight, parent_links, out_grad):
    hidden_local = hidden_states[0]
    query_local = query_rows[0]
    key_local = key_rows[0]
    grad_local = out_grad[0]
    segment_len = hidden_local.shape[0]
    key_width = key_local.shape[1]
    parent_list = lax.all_gather(parent_links, "leaf", axis=1, tiled=True)[0]
    own_index = lax.axis_index("leaf")
    ancestors = chain_slots(parent_list, own_index)
    columns = hidden_local
    values = jnp.dot(
        columns,
        lax.all_gather(value_weight, ("leaf", "grp"), axis=0, tiled=True),
        preferred_element_type=jnp.float32,
    )
    values = values.astype(jnp.bfloat16)
    key_value = jnp.concatenate([key_local, values], axis=1)
    every_segment = lax.all_gather(key_value, "leaf", axis=0, tiled=True)
    fetched = jnp.concatenate(
        [
            lax.dynamic_slice_in_dim(
                every_segment, jnp.maximum(ancestors[i], 0) * segment_len, segment_len, 0
            )
            for i in range(3)
        ],
        axis=0,
    )
    gathered = jnp.concatenate([fetched, key_value], axis=0)
    output, query_grad, grad_term = segment_pass(
        query_local,
        gathered[:, :key_width],
        gathered[:, key_width:],
        grad_local,
        key_mask(ancestors, segment_len),
    )
    grad_low = grad_term.astype(jnp.bfloat16)
    owners = jnp.concatenate([ancestors, own_index[None]])
    grad_wide = grad_low.astype(jnp.float32)
    targets = (
        owners[:, None] * segment_len + jnp.arange(segment_len, dtype=jnp.int32)[None, :]
    ).reshape(-1)
    keep_rows = (
        jnp.repeat(owners >= 0, segment_len)
        & (targets >= 0)
        & (targets < segment_len * lax.axis_size("leaf"))
    )
    targets = jnp.where(keep_rows, targets, segment_len * lax.axis_size("leaf"))
    sums = lax.psum_scatter(
        jnp.zeros((segment_len * lax.axis_size("leaf"), grad_wide.shape[1]), grad_wide.dtype)
        .at[targets]
        .add(grad_wide, mode="drop")
        .astype(jnp.bfloat16),
        "leaf",
        scatter_dimension=0,
        tiled=True,
    ).astype(jnp.float32)
    key_grad = sums[:, :key_width].astype(jnp.bfloat16)
    value_grad = sums[:, key_width:].astype(jnp.bfloat16)
    columns = hidden_local
    weight_grad = lax.psum_scatter(
        lax.dot_general(
            columns, value_grad, (((0,), (0,)), ((), ())), preferred_element_type=jnp.float32
        ),
        ("leaf", "grp"),
        scatter_dimension=0,
        tiled=True,
    )
    hidden_grad = lax.dot_general(
        value_grad,
        lax.all_gather(value_weight, ("leaf", "grp"), axis=0, tiled=True),
        (((1,), (1,)), ((), ())),
        preferred_element_type=jnp.float32,
    )
    hidden_grad = hidden_grad.astype(jnp.bfloat16)
    return (output[None], query_grad[None], key_grad[None], hidden_grad[None], weight_grad)


def solution(mesh):
    placed = (
        P("grp", "leaf", None),
        P("grp", "leaf", None),
        P("grp", "leaf", None),
        P(("leaf", "grp"), None),
        P("grp", "leaf"),
        P("grp", "leaf", None),
    )
    n_leaf, n_grp = mesh.shape["leaf"], mesh.shape["grp"]

    def body(hidden_states, query_rows, key_rows, value_weight, parent_links, out_grad):
        args = (hidden_states, query_rows, key_rows, value_weight, parent_links, out_grad)
        if n_leaf % NX == 0 and n_grp == 2 * NC and value_weight.shape[0] % 16 == 0:
            return fast_shards(n_leaf, n_grp, *args)
        return shards(*args)

    return jax.shard_map(
        body,
        mesh=mesh,
        in_specs=placed,
        out_specs=(
            P("grp", "leaf", None),
            P("grp", "leaf", None),
            P("grp", "leaf", None),
            P("grp", "leaf", None),
            P(("leaf", "grp"), None),
        ),
        check_vma=False,
    )
```

```python
import functools

import jax
import jax.numpy as jnp
from jax import lax
from jax.experimental import pallas as pl
from jax.experimental.pallas import tpu as pltpu
from jax.sharding import PartitionSpec as P

HQ = 40
HK = 4
DH = 128
MESH = pl.DeviceIdType.MESH
NX = 2
NC = 2
VMEM_LIMIT = 56 * 1024 * 1024


def nt(a, b):
    return lax.dot_general(a, b, (((1,), (1,)), ((), ())), preferred_element_type=jnp.float32)


def nn(a, b):
    return jnp.dot(a, b, preferred_element_type=jnp.float32)


def place():
    leaf = lax.axis_index("leaf")
    grp = lax.axis_index("grp")
    return leaf, grp, leaf // NX, leaf % NX, grp // NC, grp % NC


def remote(src, dst, send, recv, leaf, grp):
    return pltpu.make_async_remote_copy(
        src_ref=src,
        dst_ref=dst,
        send_sem=send,
        recv_sem=recv,
        device_id=(leaf, grp),
        device_id_type=MESH,
    )


def greet(leaf, grp, n_leaf, n_grp):
    barrier = pltpu.get_barrier_semaphore()
    for step in range(1, n_leaf):
        pl.semaphore_signal(
            barrier, inc=1, device_id=(lax.rem(leaf + step, n_leaf), grp), device_id_type=MESH
        )
    for step in range(1, n_grp):
        pl.semaphore_signal(
            barrier, inc=1, device_id=(leaf, lax.rem(grp + step, n_grp)), device_id_type=MESH
        )
    pl.semaphore_wait(barrier, n_leaf + n_grp - 2)


def ancestors_of(par, own):
    first = par[own, 0]
    second = jnp.where(first >= 0, par[jnp.maximum(first, 0), 0], -1)
    third = jnp.where(second >= 0, par[jnp.maximum(second, 0), 0], -1)
    return first, second, third


def tree_kernel(
    n_leaf, n_grp,
    parent_ref, w_ref, key_ref, hidden_ref, q_hbm, g_hbm,
    out_ref, dq_ref, dkey, dhidden, dweight,
    q_ref, g_ref, hidden_t, w_all, key_all, v0, v1, v2, v3, parents, own_parent, par, bias, probs, terms,
    x_out, x_in, z_out, z_in, acc, hid_all, dv_all, px_out, px_in, pz_out, pz_in,
    load_sem, par_send, par_recv, wz_send, wz_recv, w_send, w_recv, c_send, c_recv,
    kz_send, kz_recv, kx_send, kx_recv, vz_send, vz_recv, vx_send, vx_recv,
    gx_send, gx_recv, gz_send, gz_recv, h_send, h_recv, d_send, d_recv,
    px_send, px_recv, pz_send, pz_recv,
):
    leaf, grp, z, x, y, c = place()
    nz = n_leaf // NX
    seg = key_ref.shape[0]
    f32, bf16 = jnp.float32, jnp.bfloat16
    scale = 1.0 / DH**0.5
    fold = scale * 1.4426950408889634
    x_peer, y_peer, c_peer = z * NX + (1 - x), (1 - y) * NC + c, y * NC + (1 - c)
    values = (v0, v1, v2, v3)
    half = w_ref.shape[1] // 2
    pending = []

    loads = [
        pltpu.make_async_copy(q_hbm, q_ref, load_sem.at[0]),
        pltpu.make_async_copy(g_hbm, g_ref, load_sem.at[1]),
    ]
    for load in loads:
        load.start()
    own_parent[...] = jnp.full(own_parent.shape, parent_ref[0, 0], jnp.int32)
    greet(leaf, grp, n_leaf, n_grp)

    def start(copy):
        copy.start()
        pending.append(copy)
        return copy

    def w_over_z(part):
        lanes = pl.ds(part * half, half)
        copies = []
        for d in range(1, nz):
            copies.append(
                start(
                    remote(
                        w_ref.at[:, lanes], w_all.at[z, x, y, c, :, lanes],
                        wz_send.at[part, d - 1], wz_recv.at[part, d - 1], lax.rem(z + d, nz) * NX + x, grp,
                    )
                )
            )
        return copies

    wz = w_over_z(0)
    links = []
    for d in range(1, n_leaf):
        to = lax.rem(leaf + d, n_leaf)
        links.append(
            start(remote(own_parent, parents.at[leaf], par_send.at[d - 1], par_recv.at[d - 1], to, grp))
        )
    w_all[z, x, y, c] = w_ref[...]
    key_all[leaf] = key_ref[...]
    parents[leaf] = own_parent[...]

    def up_copy(block, whole, sems, d):
        return remote(block, whole.at[leaf], sems[0].at[d - 1], sems[1].at[d - 1], leaf + d * NX, grp)

    def up_start(block, whole, sems):
        for d in range(1, nz):
            @pl.when(z + d < nz)
            def _(d=d):
                up_copy(block, whole, sems, d).start()

    def across_own(block, whole, sems):
        @pl.when(x == 0)
        def _():
            remote(block, whole.at[leaf], sems[0].at[0], sems[1].at[0], x_peer, grp).start()

    def across_copy(whole, sems, d):
        slot = leaf - d * NX
        return remote(whole.at[slot], whole.at[slot], sems[0].at[d], sems[1].at[d], x_peer, grp)

    def across_start(whole, up_sems, sems):
        for d in range(1, nz):
            @pl.when(z - d >= 0)
            def _(d=d):
                slot = leaf - d * NX
                remote(whole.at[slot], whole.at[slot], up_sems[0].at[d - 1], up_sems[1].at[d - 1], leaf, grp).wait_recv()
                across_copy(whole, sems, d).start()

    def across_ready(block, whole, sems):
        for d in range(1, nz):
            @pl.when(z - d >= 0)
            def _(d=d):
                slot = x_peer - d * NX
                remote(whole.at[slot], whole.at[slot], sems[0].at[d], sems[1].at[d], x_peer, grp).wait_recv()

        @pl.when(x == 1)
        def _():
            remote(block, whole.at[x_peer], sems[0].at[0], sems[1].at[0], x_peer, grp).wait_recv()

    def sent(block, whole, up_sems, sems):
        for d in range(1, nz):
            @pl.when(z + d < nz)
            def _(d=d):
                up_copy(block, whole, up_sems, d).wait_send()

            @pl.when(z - d >= 0)
            def _(d=d):
                across_copy(whole, sems, d).wait_send()

        @pl.when(x == 0)
        def _():
            remote(block, whole.at[leaf], sems[0].at[0], sems[1].at[0], x_peer, grp).wait_send()

    k_up, k_across = (kz_send, kz_recv), (kx_send, kx_recv)

    rows = hidden_t.shape[3]
    for first in range(nz):
        block = NX * n_grp * rows
        turned = hidden_ref[:, first * block : (first + 1) * block].T
        for i in range(NX):
            for j in range(n_grp):
                at = (i * n_grp + j) * rows
                hidden_t[j, i, first] = turned[at : at + rows]

    quarter = half // 2
    to_core = [[], []]

    def lanes_of(part):
        return pl.ds(part * half, quarter), pl.ds(part * half + quarter, quarter)

    def w_copy(part, i, block, leaf_to, grp_to):
        return start(remote(block, block, w_send.at[part, i], w_recv.at[part, i], leaf_to, grp_to))

    def w_core(part, i, block):
        to_core[part].append(
            start(remote(block, block, c_send.at[part, i], c_recv.at[part, i], leaf, c_peer))
        )

    def w_first(part):
        a, b = lanes_of(part)
        return (
            w_copy(part, 0, w_all.at[:, x, y, c, :, a], x_peer, grp),
            w_copy(part, 1, w_all.at[:, x, y, c, :, b], leaf, y_peer),
        )

    def w_second(part, first):
        a, b = lanes_of(part)
        first[0].wait_recv()
        over_y = w_copy(part, 2, w_all.at[:, :, y, c, :, a], leaf, y_peer)
        first[1].wait_recv()
        over_x = w_copy(part, 3, w_all.at[:, x, :, c, :, b], x_peer, grp)
        w_core(part, 0, w_all.at[:, x, y, c, :, pl.ds(part * half, half)])
        w_core(part, 1, w_all.at[:, 1 - x, y, c, :, a])
        w_core(part, 2, w_all.at[:, x, 1 - y, c, :, b])
        return over_y, over_x

    def w_third(part, second):
        a, b = lanes_of(part)
        second[0].wait_recv()
        w_core(part, 3, w_all.at[:, :, 1 - y, c, :, a])
        second[1].wait_recv()
        w_core(part, 4, w_all.at[:, 1 - x, :, c, :, b])

    def v_sems(h):
        return (vz_send.at[h], vz_recv.at[h]), (vx_send.at[h], vx_recv.at[h])

    def project(part):
        for copy in to_core[part]:
            copy.wait_recv()
        weight = w_all[:, :, :, :, :, part * half : (part + 1) * half].reshape(hidden_ref.shape[1], half)
        pair = nn(hidden_ref[...], weight).astype(bf16)
        for i in range(HK // 2):
            h = part * (HK // 2) + i
            whole = values[h]
            whole[leaf] = pair[:, i * DH : (i + 1) * DH]
            up, across = v_sems(h)
            up_start(whole.at[leaf], whole, up)
            across_own(whole.at[leaf], whole, across)

    for copy in wz:
        copy.wait_recv()
    first0 = w_first(0)
    wz = w_over_z(1)
    second0 = w_second(0, first0)
    for copy in wz:
        copy.wait_recv()
    first1 = w_first(1)
    up_start(key_ref, key_all, k_up)
    w_third(0, second0)
    second1 = w_second(1, first1)
    project(0)
    w_third(1, second1)
    across_own(key_ref, key_all, k_across)
    across_start(key_all, k_up, k_across)
    hidden = []
    for d in range(1, n_grp):
        to = lax.rem(grp + d, n_grp)
        hidden.append(
            start(remote(hidden_t.at[to], hid_all.at[d], h_send.at[d - 1], h_recv.at[d - 1], leaf, to))
        )
    project(1)
    for copy in links:
        copy.wait_recv()
    listing = pltpu.make_async_copy(parents.at[:, 0], par, load_sem.at[2])
    listing.start()

    def forward(h):
        if h < HK:
            up, across = v_sems(h)
            across_start(values[h], up, across)

    listing.wait()
    chain = ancestors_of(par, leaf)
    for i in range(3):
        bias[i * seg : (i + 1) * seg, :] = jnp.full(
            (seg, 2 * seg), jnp.where(chain[i] >= 0, 0.0, -1e30), f32
        )
    col = lax.broadcasted_iota(jnp.int32, (seg, 2 * seg), 0)
    row = lax.broadcasted_iota(jnp.int32, (seg, 2 * seg), 1)
    row = jnp.where(row >= seg, row - seg, row)
    bias[3 * seg :, :] = jnp.where(col <= row, 0.0, -1e30)
    across_ready(key_ref, key_all, k_across)
    for load in loads:
        load.wait()

    groups = HQ // HK
    slots = [jnp.maximum(chain[i], 0) for i in range(3)] + [leaf]

    def places(h, pair):
        at = (h * groups + 2 * pair) * DH
        return slice(at, at + DH), slice(at + DH, at + 2 * DH)

    def keys_of(h):
        return jnp.concatenate([key_all[slot, :, h * DH : (h + 1) * DH] for slot in slots], axis=0)

    def softmax(h):
        key = keys_of(h)
        for pair in range(groups // 2):
            one, two = places(h, pair)
            q = jnp.concatenate([q_ref[:, one], q_ref[:, two]], axis=0)
            s = nt(key, q) * fold + bias[...]
            e = jnp.exp2(s - jnp.max(s, axis=0, keepdims=True))
            probs[h * (groups // 2) + pair] = e * (1.0 / jnp.sum(e, axis=0, keepdims=True))

    def gradients(h):
        up, across = v_sems(h)
        across_ready(values[h].at[leaf], values[h], across)
        value = jnp.concatenate([values[h][slot] for slot in slots], axis=0)
        key_t = keys_of(h).T
        value_t = value.T
        dk = jnp.zeros((4 * seg, DH), f32)
        dv = jnp.zeros((4 * seg, DH), f32)
        for pair in range(groups // 2):
            one, two = places(h, pair)
            q = jnp.concatenate([q_ref[:, one], q_ref[:, two]], axis=0)
            g = jnp.concatenate([g_ref[:, one], g_ref[:, two]], axis=0)
            p = probs[h * (groups // 2) + pair]
            p_low = p.astype(bf16)
            dp = nt(value, g)
            delta = jnp.sum(p * dp, axis=0, keepdims=True)
            ds = (p * (dp - delta)).astype(bf16)
            o = nn(value_t, p_low).T.astype(bf16)
            out_ref[:, one] = o[:seg]
            out_ref[:, two] = o[seg:]
            dq = (nn(key_t, ds) * scale).T.astype(bf16)
            dq_ref[:, one] = dq[:seg]
            dq_ref[:, two] = dq[seg:]
            dk = dk + nn(ds, q)
            dv = dv + nn(p_low, g)
        for i in range(4):
            terms[h, i] = dv[i * seg : (i + 1) * seg].astype(bf16)
            terms[HK + h, i] = (dk[i * seg : (i + 1) * seg] * scale).astype(bf16)

    def term(m, target):
        slot = jnp.where(chain[0] == target, 0, jnp.where(chain[1] == target, 1, 2))
        hit = (chain[0] == target) | (chain[1] == target) | (chain[2] == target)
        block = terms[m, slot]
        return jnp.where(hit, block, jnp.zeros_like(block))

    def x_copy(m, t):
        return remote(x_out.at[m, t], x_in.at[m, t], gx_send.at[m, t], gx_recv.at[m, t], x_peer, grp)

    def z_copy(m, t):
        return remote(z_out.at[m, t], z_in.at[m, z], gz_send.at[m, t], gz_recv.at[m, z], t * NX + x, grp)

    def x_stage(m):
        for t in range(nz):
            @pl.when((t < z) | ((t == z) & (x == 1)))
            def _(t=t):
                x_out[m, t] = term(m, t * NX + (1 - x))
                x_copy(m, t).start()

    def z_stage(m):
        for t in range(nz - 1):
            @pl.when(t < z)
            def _(t=t):
                x_copy(m, t).wait_recv()
                total = term(m, t * NX + x).astype(f32) + x_in[m, t].astype(f32)
                z_out[m, t] = total.astype(bf16)
                z_copy(m, t).start()

    def owned(m):
        acc[...] = terms[m, 3].astype(f32)
        for t in range(nz):
            @pl.when((t == z) & (x == 0))
            def _(t=t):
                x_copy(m, t).wait_recv()
                acc[...] += x_in[m, t].astype(f32)

        for t in range(1, nz):
            @pl.when(t > z)
            def _(t=t):
                block = z_in.at[m, t]
                remote(block, block, gz_send.at[m, t], gz_recv.at[m, t], t * NX + x, grp).wait_recv()
                acc[...] += z_in[m, t].astype(f32)

        h = m % HK
        if m < HK:
            dv_all[h // 2, grp, :, (h % 2) * DH : (h % 2 + 1) * DH] = acc[...].astype(bf16)
        else:
            dkey[:, h * DH : (h + 1) * DH] = acc[...].astype(bf16)

    def spread(part):
        mine = dv_all.at[part, grp]
        to_y = start(remote(mine, mine, d_send.at[part, 0], d_recv.at[part, 0], leaf, y_peer))
        to_c = start(remote(mine, mine, d_send.at[part, 1], d_recv.at[part, 1], leaf, c_peer))
        return to_y, to_c

    def relay(part, to_y):
        to_y.wait_recv()
        theirs = dv_all.at[part, y_peer]
        return start(remote(theirs, theirs, d_send.at[part, 2], d_recv.at[part, 2], leaf, c_peer))

    def partials(part, side):
        total = nn(hidden_t[grp, side].reshape(nz * rows, seg), dv_all[part, grp])
        for d in range(1, n_grp):
            owner = lax.rem(grp + n_grp - d, n_grp)
            total = total + nn(hid_all[d, side].reshape(nz * rows, seg), dv_all[part, owner])
        return total

    def px_copy(part):
        return remote(px_out.at[part], px_in.at[part], px_send.at[part], px_recv.at[part], x_peer, grp)

    def weight_x(part):
        total = partials(part, 1 - x).astype(bf16)
        px_out[part] = total.reshape(nz, rows, half)
        start(px_copy(part))
        pz_out[part] = partials(part, x).reshape(nz, rows, half)

    def weight_z(part):
        px_copy(part).wait_recv()
        copies = []
        for d in range(1, nz):
            t = lax.rem(z + d, nz)
            px_out_z = pz_out[part, t] + px_in[part, t].astype(f32)
            pz_in[part, 0, d - 1] = px_out_z.astype(bf16)
            copies.append(
                start(
                    remote(
                        pz_in.at[part, 0, d - 1], pz_in.at[part, 1, d - 1],
                        pz_send.at[part, d - 1], pz_recv.at[part, d - 1], t * NX + x, grp,
                    )
                )
            )
        return copies

    for h in range(HK):
        softmax(h)
        forward(h)
    for h in range(HK):
        gradients(h)
        x_stage(h)
        if h > 0:
            z_stage(h - 1)
    z_stage(HK - 1)
    for h in range(HK):
        x_stage(HK + h)
    owned(0)
    owned(1)
    to_y, to_c = spread(0)
    for copy in hidden:
        copy.wait_recv()
    relayed = relay(0, to_y)
    z_stage(HK)
    to_c.wait_recv()
    relayed.wait_recv()
    weight_x(0)
    owned(2)
    owned(3)
    to_y, to_c = spread(1)
    z_stage(HK + 1)
    relayed = relay(1, to_y)
    z_stage(HK + 2)
    to_c.wait_recv()
    relayed.wait_recv()
    weight_x(1)
    z_stage(HK + 3)
    copies = weight_z(0)
    width = hidden_ref.shape[1] // 4
    weight = w_all[...].reshape(hidden_ref.shape[1], w_ref.shape[1])
    dv_low = jnp.concatenate([dv_all[0, grp], dv_all[1, grp]], axis=1)
    for i in range(4):
        dhidden[:, i * width : (i + 1) * width] = nt(dv_low, weight[i * width : (i + 1) * width, :]).astype(bf16)
    copies += weight_z(1)
    for h in range(HK):
        owned(HK + h)
    for copy in copies:
        copy.wait_recv()
    for part in range(2):
        total = pz_out[part, z] + px_in[part, z].astype(f32)
        for d in range(1, nz):
            total = total + pz_in[part, 1, d - 1].astype(f32)
        dweight[:, part * half : (part + 1) * half] = total

    sent(key_ref, key_all, k_up, k_across)
    for h in range(HK):
        up, across = v_sems(h)
        sent(values[h].at[leaf], values[h], up, across)
    for m in range(2 * HK):
        for t in range(nz):
            @pl.when((t < z) | ((t == z) & (x == 1)))
            def _(t=t, m=m):
                x_copy(m, t).wait_send()
        for t in range(nz - 1):
            @pl.when(t < z)
            def _(t=t, m=m):
                z_copy(m, t).wait_send()
    for copy in pending:
        copy.wait_send()


def fast_shards(n_leaf, n_grp, hidden_states, query_rows, key_rows, value_weight, parent_links, out_grad):
    hidden, q, g, key = hidden_states[0], query_rows[0], out_grad[0], key_rows[0]
    rows, width = value_weight.shape
    seg, features = hidden.shape
    nz, ny = n_leaf // NX, n_grp // NC
    half = width // 2
    bf16, f32 = jnp.bfloat16, jnp.float32
    vmem = pl.BlockSpec(memory_space=pltpu.VMEM)
    anywhere = pl.BlockSpec(memory_space=pl.ANY)
    held, dma = pltpu.VMEM, pltpu.SemaphoreType.DMA
    pairs = lambda *dims: [dma(dims)] * 2
    out, dq, dkey, dhidden, dweight = pl.pallas_call(
        functools.partial(tree_kernel, n_leaf, n_grp),
        out_shape=[
            jax.ShapeDtypeStruct(q.shape, bf16),
            jax.ShapeDtypeStruct(q.shape, bf16),
            jax.ShapeDtypeStruct(key.shape, bf16),
            jax.ShapeDtypeStruct(hidden.shape, bf16),
            jax.ShapeDtypeStruct(value_weight.shape, f32),
        ],
        in_specs=[pl.BlockSpec(memory_space=pltpu.SMEM)] + [vmem] * 3 + [anywhere] * 2,
        out_specs=[vmem] * 5,
        scratch_shapes=[
            held(q.shape, bf16),
            held(q.shape, bf16),
            held((n_grp, NX, nz, rows, seg), bf16),
            held((nz, NX, ny, NC, rows, width), bf16),
            held((n_leaf, seg, width), bf16),
        ]
        + [held((n_leaf, seg, DH), bf16)] * HK
        + [
            held((n_leaf, 8, 128), jnp.int32),
            held((8, 128), jnp.int32),
            pltpu.SMEM((n_leaf, 128), jnp.int32),
            held((4 * seg, 2 * seg), f32),
            held((HQ // 2, 4 * seg, 2 * seg), f32),
            held((2 * HK, 4, seg, DH), bf16),
        ]
        + [held((2 * HK, nz, seg, DH), bf16)] * 4
        + [
            held((seg, DH), f32),
            held((n_grp, NX, nz, rows, seg), bf16),
            held((2, n_grp, seg, half), bf16),
            held((2, nz, rows, half), bf16),
            held((2, nz, rows, half), bf16),
            held((2, nz, rows, half), f32),
            held((2, 2, nz - 1, rows, half), bf16),
            dma((3,)),
        ]
        + pairs(n_leaf - 1)
        + pairs(2, nz - 1)
        + pairs(2, 4)
        + pairs(2, 5)
        + pairs(nz - 1)
        + pairs(nz)
        + pairs(HK, nz - 1)
        + pairs(HK, nz)
        + pairs(2 * HK, nz) * 2
        + pairs(n_grp - 1)
        + pairs(2, 3)
        + pairs(2)
        + pairs(2, nz - 1),
        compiler_params=pltpu.CompilerParams(
            collective_id=0, has_side_effects=True, vmem_limit_bytes=VMEM_LIMIT
        ),
        cost_estimate=pl.CostEstimate(
            flops=12 * HQ * seg * 4 * seg * DH + 6 * seg * features * width,
            bytes_accessed=10000000,
            transcendentals=HQ * seg * 4 * seg,
        ),
    )(parent_links, value_weight, key, hidden, q, g)
    return out[None], dq[None], dkey[None], dhidden[None], dweight


def chain_slots(parent_list, own_index):
    total = parent_list.shape[0]

    def parent_of(node_index):
        hit = jnp.arange(total, dtype=jnp.int32) == node_index
        found = jnp.sum(jnp.where(hit, parent_list, 0))
        return jnp.where(node_index >= 0, found, -1)

    first = parent_of(own_index)
    second = parent_of(first)
    third = parent_of(second)
    return jnp.stack([first, second, third])


def key_mask(ancestors, segment_len):
    valid = jnp.concatenate([ancestors >= 0, jnp.ones((1,), bool)])
    block_ok = jnp.repeat(valid, segment_len)[None, :]
    row_ids = jnp.arange(segment_len, dtype=jnp.int32)[:, None]
    col_ids = jnp.arange(4 * segment_len, dtype=jnp.int32)[None, :]
    causal = (col_ids < 3 * segment_len) | (col_ids - 3 * segment_len <= row_ids)
    return block_ok & causal


def segment_pass(query_seg, key_all, value_all, grad_seg, visible):
    segment_len = query_seg.shape[0]
    groups = HQ // HK
    scale_factor = 1.0 / DH**0.5
    query_heads = query_seg.reshape(segment_len, HK, groups, DH)
    key_heads = key_all.reshape(-1, HK, DH)
    value_heads = value_all.reshape(-1, HK, DH)
    grad_heads = grad_seg.reshape(segment_len, HK, groups, DH)
    scores = (
        jnp.einsum("rhgd,khd->hgrk", query_heads, key_heads, preferred_element_type=jnp.float32)
        * scale_factor
    )
    scores = jnp.where(visible, scores, -1e30)
    row_max = jnp.max(scores, axis=-1, keepdims=True)
    weights_exp = jnp.where(visible, jnp.exp(scores - row_max), 0.0)
    probs = weights_exp / jnp.sum(weights_exp, axis=-1, keepdims=True)
    probs_low = probs.astype(jnp.bfloat16)
    output = jnp.einsum(
        "hgrk,khd->rhgd", probs_low, value_heads, preferred_element_type=jnp.float32
    )
    output = output.reshape(segment_len, HQ * DH).astype(jnp.bfloat16)
    dprobs = jnp.einsum(
        "rhgd,khd->hgrk", grad_heads, value_heads, preferred_element_type=jnp.float32
    )
    delta = jnp.sum(probs * dprobs, axis=-1, keepdims=True)
    dscores = (probs * (dprobs - delta)).astype(jnp.bfloat16)
    query_grad = (
        jnp.einsum("hgrk,khd->rhgd", dscores, key_heads, preferred_element_type=jnp.float32)
        * scale_factor
    )
    query_grad = query_grad.reshape(segment_len, HQ * DH).astype(jnp.bfloat16)
    key_part = (
        jnp.einsum("hgrk,rhgd->khd", dscores, query_heads, preferred_element_type=jnp.float32)
        * scale_factor
    )
    value_part = jnp.einsum(
        "hgrk,rhgd->khd", probs_low, grad_heads, preferred_element_type=jnp.float32
    )
    grad_term = jnp.concatenate(
        [key_part.reshape(-1, HK * DH), value_part.reshape(-1, HK * DH)], axis=1
    )
    return (output, query_grad, grad_term)


def shards(hidden_states, query_rows, key_rows, value_weight, parent_links, out_grad):
    hidden_local = hidden_states[0]
    query_local = query_rows[0]
    key_local = key_rows[0]
    grad_local = out_grad[0]
    segment_len = hidden_local.shape[0]
    key_width = key_local.shape[1]
    parent_list = lax.all_gather(parent_links, "leaf", axis=1, tiled=True)[0]
    own_index = lax.axis_index("leaf")
    ancestors = chain_slots(parent_list, own_index)
    columns = hidden_local
    values = jnp.dot(
        columns,
        lax.all_gather(value_weight, ("leaf", "grp"), axis=0, tiled=True),
        preferred_element_type=jnp.float32,
    )
    values = values.astype(jnp.bfloat16)
    key_value = jnp.concatenate([key_local, values], axis=1)
    every_segment = lax.all_gather(key_value, "leaf", axis=0, tiled=True)
    fetched = jnp.concatenate(
        [
            lax.dynamic_slice_in_dim(
                every_segment, jnp.maximum(ancestors[i], 0) * segment_len, segment_len, 0
            )
            for i in range(3)
        ],
        axis=0,
    )
    gathered = jnp.concatenate([fetched, key_value], axis=0)
    output, query_grad, grad_term = segment_pass(
        query_local,
        gathered[:, :key_width],
        gathered[:, key_width:],
        grad_local,
        key_mask(ancestors, segment_len),
    )
    grad_low = grad_term.astype(jnp.bfloat16)
    owners = jnp.concatenate([ancestors, own_index[None]])
    grad_wide = grad_low.astype(jnp.float32)
    targets = (
        owners[:, None] * segment_len + jnp.arange(segment_len, dtype=jnp.int32)[None, :]
    ).reshape(-1)
    keep_rows = (
        jnp.repeat(owners >= 0, segment_len)
        & (targets >= 0)
        & (targets < segment_len * lax.axis_size("leaf"))
    )
    targets = jnp.where(keep_rows, targets, segment_len * lax.axis_size("leaf"))
    sums = lax.psum_scatter(
        jnp.zeros((segment_len * lax.axis_size("leaf"), grad_wide.shape[1]), grad_wide.dtype)
        .at[targets]
        .add(grad_wide, mode="drop")
        .astype(jnp.bfloat16),
        "leaf",
        scatter_dimension=0,
        tiled=True,
    ).astype(jnp.float32)
    key_grad = sums[:, :key_width].astype(jnp.bfloat16)
    value_grad = sums[:, key_width:].astype(jnp.bfloat16)
    columns = hidden_local
    weight_grad = lax.psum_scatter(
        lax.dot_general(
            columns, value_grad, (((0,), (0,)), ((), ())), preferred_element_type=jnp.float32
        ),
        ("leaf", "grp"),
        scatter_dimension=0,
        tiled=True,
    )
    hidden_grad = lax.dot_general(
        value_grad,
        lax.all_gather(value_weight, ("leaf", "grp"), axis=0, tiled=True),
        (((1,), (1,)), ((), ())),
        preferred_element_type=jnp.float32,
    )
    hidden_grad = hidden_grad.astype(jnp.bfloat16)
    return (output[None], query_grad[None], key_grad[None], hidden_grad[None], weight_grad)


def solution(mesh):
    placed = (
        P("grp", "leaf", None),
        P("grp", "leaf", None),
        P("grp", "leaf", None),
        P(("leaf", "grp"), None),
        P("grp", "leaf"),
        P("grp", "leaf", None),
    )
    n_leaf, n_grp = mesh.shape["leaf"], mesh.shape["grp"]

    def body(hidden_states, query_rows, key_rows, value_weight, parent_links, out_grad):
        args = (hidden_states, query_rows, key_rows, value_weight, parent_links, out_grad)
        if n_leaf % NX == 0 and n_grp == 2 * NC and value_weight.shape[0] % 16 == 0:
            return fast_shards(n_leaf, n_grp, *args)
        return shards(*args)

    return jax.shard_map(
        body,
        mesh=mesh,
        in_specs=placed,
        out_specs=(
            P("grp", "leaf", None),
            P("grp", "leaf", None),
            P("grp", "leaf", None),
            P("grp", "leaf", None),
            P(("leaf", "grp"), None),
        ),
        check_vma=False,
    )
```

```python
import functools

import jax
import jax.numpy as jnp
from jax import lax
from jax.experimental import pallas as pl
from jax.experimental.pallas import tpu as pltpu
from jax.sharding import PartitionSpec as P

HQ = 40
HK = 4
DH = 128
MESH = pl.DeviceIdType.MESH
NX = 2
NC = 2
VMEM_LIMIT = 56 * 1024 * 1024


def nt(a, b):
    return lax.dot_general(a, b, (((1,), (1,)), ((), ())), preferred_element_type=jnp.float32)


def nn(a, b):
    return jnp.dot(a, b, preferred_element_type=jnp.float32)


def place():
    leaf = lax.axis_index("leaf")
    grp = lax.axis_index("grp")
    return leaf, grp, leaf // NX, leaf % NX, grp // NC, grp % NC


def remote(src, dst, send, recv, leaf, grp):
    return pltpu.make_async_remote_copy(
        src_ref=src,
        dst_ref=dst,
        send_sem=send,
        recv_sem=recv,
        device_id=(leaf, grp),
        device_id_type=MESH,
    )


def greet(leaf, grp, n_leaf, n_grp):
    barrier = pltpu.get_barrier_semaphore()
    for step in range(1, n_leaf):
        pl.semaphore_signal(
            barrier, inc=1, device_id=(lax.rem(leaf + step, n_leaf), grp), device_id_type=MESH
        )
    for step in range(1, n_grp):
        pl.semaphore_signal(
            barrier, inc=1, device_id=(leaf, lax.rem(grp + step, n_grp)), device_id_type=MESH
        )
    pl.semaphore_wait(barrier, n_leaf + n_grp - 2)


def ancestors_of(par, own):
    first = par[own, 0]
    second = jnp.where(first >= 0, par[jnp.maximum(first, 0), 0], -1)
    third = jnp.where(second >= 0, par[jnp.maximum(second, 0), 0], -1)
    return first, second, third


def tree_kernel(
    n_leaf, n_grp,
    parent_ref, w_ref, key_ref, hidden_ref, q_hbm, g_hbm,
    out_hbm, dq_hbm, dkey, dhidden, dweight,
    q_ref, g_ref, out_ref, dq_ref, hidden_t, w_all, k0, k1, k2, k3, v0, v1, v2, v3, parents, own_parent, par, bias, probs, terms,
    x_out, x_in, z_out, z_in, acc, hid_all, dv_all, px_out, px_in, pz_out, pz_in,
    load_sem, store_sem, par_send, par_recv, wz_send, wz_recv, w_send, w_recv, c_send, c_recv,
    kz_send, kz_recv, kx_send, kx_recv, vz_send, vz_recv, vx_send, vx_recv,
    gx_send, gx_recv, gz_send, gz_recv, h_send, h_recv, d_send, d_recv,
    px_send, px_recv, pz_send, pz_recv,
):
    leaf, grp, z, x, y, c = place()
    nz = n_leaf // NX
    seg = key_ref.shape[0]
    f32, bf16 = jnp.float32, jnp.bfloat16
    scale = 1.0 / DH**0.5
    fold = scale * 1.4426950408889634
    x_peer, y_peer, c_peer = z * NX + (1 - x), (1 - y) * NC + c, y * NC + (1 - c)
    keys, values = (k0, k1, k2, k3), (v0, v1, v2, v3)
    half = w_ref.shape[1] // 2
    pending = []

    loads = [
        pltpu.make_async_copy(q_hbm, q_ref, load_sem.at[0]),
        pltpu.make_async_copy(g_hbm, g_ref, load_sem.at[1]),
    ]
    for load in loads:
        load.start()
    own_parent[...] = jnp.full(own_parent.shape, parent_ref[0, 0], jnp.int32)
    greet(leaf, grp, n_leaf, n_grp)

    def start(copy):
        copy.start()
        pending.append(copy)
        return copy

    def w_over_z(part):
        copies = []
        two = pl.ds(2 * part, 2)
        for d in range(1, nz):
            copies.append(
                start(
                    remote(
                        w_all.at[two, z, x, y, c], w_all.at[two, z, x, y, c],
                        wz_send.at[part, d - 1], wz_recv.at[part, d - 1], lax.rem(z + d, nz) * NX + x, grp,
                    )
                )
            )
        return copies

    quarter = half // 2
    for i in range(4):
        w_all[i, z, x, y, c] = w_ref[:, i * quarter : (i + 1) * quarter]
    wz = w_over_z(0)
    links = []
    for d in range(1, n_leaf):
        to = lax.rem(leaf + d, n_leaf)
        links.append(
            start(remote(own_parent, parents.at[leaf], par_send.at[d - 1], par_recv.at[d - 1], to, grp))
        )
    for h in range(HK):
        keys[h][leaf] = key_ref[:, h * DH : (h + 1) * DH]
    parents[leaf] = own_parent[...]

    def up_copy(block, whole, sems, d):
        return remote(block, whole.at[leaf], sems[0].at[d - 1], sems[1].at[d - 1], leaf + d * NX, grp)

    def up_start(block, whole, sems):
        for d in range(1, nz):
            @pl.when(z + d < nz)
            def _(d=d):
                up_copy(block, whole, sems, d).start()

    def across_own(block, whole, sems):
        @pl.when(x == 0)
        def _():
            remote(block, whole.at[leaf], sems[0].at[0], sems[1].at[0], x_peer, grp).start()

    def across_copy(whole, sems, d):
        slot = leaf - d * NX
        return remote(whole.at[slot], whole.at[slot], sems[0].at[d], sems[1].at[d], x_peer, grp)

    def across_start(whole, up_sems, sems):
        for d in range(1, nz):
            @pl.when(z - d >= 0)
            def _(d=d):
                slot = leaf - d * NX
                remote(whole.at[slot], whole.at[slot], up_sems[0].at[d - 1], up_sems[1].at[d - 1], leaf, grp).wait_recv()
                across_copy(whole, sems, d).start()

    def across_ready(block, whole, sems):
        for d in range(1, nz):
            @pl.when(z - d >= 0)
            def _(d=d):
                slot = x_peer - d * NX
                remote(whole.at[slot], whole.at[slot], sems[0].at[d], sems[1].at[d], x_peer, grp).wait_recv()

        @pl.when(x == 1)
        def _():
            remote(block, whole.at[x_peer], sems[0].at[0], sems[1].at[0], x_peer, grp).wait_recv()

    def sent(block, whole, up_sems, sems):
        for d in range(1, nz):
            @pl.when(z + d < nz)
            def _(d=d):
                up_copy(block, whole, up_sems, d).wait_send()

            @pl.when(z - d >= 0)
            def _(d=d):
                across_copy(whole, sems, d).wait_send()

        @pl.when(x == 0)
        def _():
            remote(block, whole.at[leaf], sems[0].at[0], sems[1].at[0], x_peer, grp).wait_send()

    def k_sems(h):
        return (kz_send.at[h], kz_recv.at[h]), (kx_send.at[h], kx_recv.at[h])

    def k_forward(h):
        up, across = k_sems(h)
        across_own(keys[h].at[leaf], keys[h], across)
        across_start(keys[h], up, across)

    rows = hidden_t.shape[3]
    for first in range(nz):
        block = NX * n_grp * rows
        turned = hidden_ref[:, first * block : (first + 1) * block].T
        for i in range(NX):
            for j in range(n_grp):
                at = (i * n_grp + j) * rows
                hidden_t[j, i, first] = turned[at : at + rows]

    to_core = [[], []]

    def w_copy(part, i, block, leaf_to, grp_to):
        return start(remote(block, block, w_send.at[part, i], w_recv.at[part, i], leaf_to, grp_to))

    def w_core(part, i, block):
        to_core[part].append(
            start(remote(block, block, c_send.at[part, i], c_recv.at[part, i], leaf, c_peer))
        )

    def w_first(part):
        a, b = 2 * part, 2 * part + 1
        return (
            w_copy(part, 0, w_all.at[a, :, x, y, c], x_peer, grp),
            w_copy(part, 1, w_all.at[b, :, x, y, c], leaf, y_peer),
        )

    def w_second(part, first):
        a, b = 2 * part, 2 * part + 1
        first[0].wait_recv()
        over_y = w_copy(part, 2, w_all.at[a, :, :, y, c], leaf, y_peer)
        first[1].wait_recv()
        over_x = w_copy(part, 3, w_all.at[b, :, x, :, c], x_peer, grp)
        w_core(part, 0, w_all.at[pl.ds(2 * part, 2), :, x, y, c])
        w_core(part, 1, w_all.at[a, :, 1 - x, y, c])
        w_core(part, 2, w_all.at[b, :, x, 1 - y, c])
        return over_y, over_x

    def w_third(part, second):
        a, b = 2 * part, 2 * part + 1
        second[0].wait_recv()
        w_core(part, 3, w_all.at[a, :, :, 1 - y, c])
        second[1].wait_recv()
        w_core(part, 4, w_all.at[b, :, 1 - x, :, c])

    def v_sems(h):
        return (vz_send.at[h], vz_recv.at[h]), (vx_send.at[h], vx_recv.at[h])

    def project(part):
        for copy in to_core[part]:
            copy.wait_recv()
        weight = jnp.concatenate(
            [w_all[2 * part + i].reshape(hidden_ref.shape[1], quarter) for i in range(2)], axis=1
        )
        pair = nn(hidden_ref[...], weight).astype(bf16)
        for i in range(HK // 2):
            h = part * (HK // 2) + i
            whole = values[h]
            whole[leaf] = pair[:, i * DH : (i + 1) * DH]
            up, across = v_sems(h)
            up_start(whole.at[leaf], whole, up)
            across_own(whole.at[leaf], whole, across)

    for copy in wz:
        copy.wait_recv()
    first0 = w_first(0)
    wz = w_over_z(1)
    second0 = w_second(0, first0)
    for copy in wz:
        copy.wait_recv()
    first1 = w_first(1)
    for h in range(HK):
        up_start(keys[h].at[leaf], keys[h], k_sems(h)[0])
    w_third(0, second0)
    second1 = w_second(1, first1)
    project(0)
    k_forward(0)
    w_third(1, second1)
    k_forward(1)
    hidden = []
    for d in range(1, n_grp):
        to = lax.rem(grp + d, n_grp)
        hidden.append(
            start(remote(hidden_t.at[to], hid_all.at[d], h_send.at[d - 1], h_recv.at[d - 1], leaf, to))
        )
    project(1)
    k_forward(2)
    k_forward(3)
    for copy in links:
        copy.wait_recv()
    listing = pltpu.make_async_copy(parents.at[:, 0], par, load_sem.at[2])
    listing.start()

    def forward(h):
        if h < HK:
            up, across = v_sems(h)
            across_start(values[h], up, across)

    listing.wait()
    chain = ancestors_of(par, leaf)
    for i in range(3):
        bias[i * seg : (i + 1) * seg, :] = jnp.full(
            (seg, 2 * seg), jnp.where(chain[i] >= 0, 0.0, -1e30), f32
        )
    col = lax.broadcasted_iota(jnp.int32, (seg, 2 * seg), 0)
    row = lax.broadcasted_iota(jnp.int32, (seg, 2 * seg), 1)
    row = jnp.where(row >= seg, row - seg, row)
    bias[3 * seg :, :] = jnp.where(col <= row, 0.0, -1e30)
    for load in loads:
        load.wait()

    groups = HQ // HK
    slots = [jnp.maximum(chain[i], 0) for i in range(3)] + [leaf]

    def places(h, pair):
        at = (h * groups + 2 * pair) * DH
        return slice(at, at + DH), slice(at + DH, at + 2 * DH)

    def keys_of(h):
        return jnp.concatenate([keys[h][slot] for slot in slots], axis=0)

    def softmax(h):
        across_ready(keys[h].at[leaf], keys[h], k_sems(h)[1])
        key = keys_of(h)
        for pair in range(groups // 2):
            one, two = places(h, pair)
            q = jnp.concatenate([q_ref[:, one], q_ref[:, two]], axis=0)
            s = nt(key, q) * fold + bias[...]
            e = jnp.exp2(s - jnp.max(s, axis=0, keepdims=True))
            probs[h * (groups // 2) + pair] = e * (1.0 / jnp.sum(e, axis=0, keepdims=True))

    def stores(h):
        lanes = pl.ds(h * groups * DH, groups * DH)
        return (
            pltpu.make_async_copy(out_ref.at[:, lanes], out_hbm.at[:, lanes], store_sem.at[h, 0]),
            pltpu.make_async_copy(dq_ref.at[:, lanes], dq_hbm.at[:, lanes], store_sem.at[h, 1]),
        )

    def gradients(h):
        up, across = v_sems(h)
        across_ready(values[h].at[leaf], values[h], across)
        value = jnp.concatenate([values[h][slot] for slot in slots], axis=0)
        key_t = keys_of(h).T
        value_t = value.T
        dk = jnp.zeros((4 * seg, DH), f32)
        dv = jnp.zeros((4 * seg, DH), f32)
        for pair in range(groups // 2):
            one, two = places(h, pair)
            q = jnp.concatenate([q_ref[:, one], q_ref[:, two]], axis=0)
            g = jnp.concatenate([g_ref[:, one], g_ref[:, two]], axis=0)
            p = probs[h * (groups // 2) + pair]
            p_low = p.astype(bf16)
            dp = nt(value, g)
            delta = jnp.sum(p * dp, axis=0, keepdims=True)
            ds = (p * (dp - delta)).astype(bf16)
            o = nn(value_t, p_low).T.astype(bf16)
            out_ref[:, one] = o[:seg]
            out_ref[:, two] = o[seg:]
            dq = (nn(key_t, ds) * scale).T.astype(bf16)
            dq_ref[:, one] = dq[:seg]
            dq_ref[:, two] = dq[seg:]
            dk = dk + nn(ds, q)
            dv = dv + nn(p_low, g)
        for store in stores(h):
            store.start()
        for i in range(4):
            terms[h, i] = dv[i * seg : (i + 1) * seg].astype(bf16)
            terms[HK + h, i] = (dk[i * seg : (i + 1) * seg] * scale).astype(bf16)

    def term(m, target):
        slot = jnp.where(chain[0] == target, 0, jnp.where(chain[1] == target, 1, 2))
        hit = (chain[0] == target) | (chain[1] == target) | (chain[2] == target)
        block = terms[m, slot]
        return jnp.where(hit, block, jnp.zeros_like(block))

    def x_copy(m, t):
        return remote(x_out.at[m, t], x_in.at[m, t], gx_send.at[m, t], gx_recv.at[m, t], x_peer, grp)

    def z_copy(m, t):
        return remote(z_out.at[m, t], z_in.at[m, z], gz_send.at[m, t], gz_recv.at[m, z], t * NX + x, grp)

    def x_stage(m):
        for t in range(nz):
            @pl.when((t < z) | ((t == z) & (x == 1)))
            def _(t=t):
                x_out[m, t] = term(m, t * NX + (1 - x))
                x_copy(m, t).start()

    def z_stage(m):
        for t in range(nz - 1):
            @pl.when(t < z)
            def _(t=t):
                x_copy(m, t).wait_recv()
                total = term(m, t * NX + x).astype(f32) + x_in[m, t].astype(f32)
                z_out[m, t] = total.astype(bf16)
                z_copy(m, t).start()

    def owned(m):
        acc[...] = terms[m, 3].astype(f32)
        for t in range(nz):
            @pl.when((t == z) & (x == 0))
            def _(t=t):
                x_copy(m, t).wait_recv()
                acc[...] += x_in[m, t].astype(f32)

        for t in range(1, nz):
            @pl.when(t > z)
            def _(t=t):
                block = z_in.at[m, t]
                remote(block, block, gz_send.at[m, t], gz_recv.at[m, t], t * NX + x, grp).wait_recv()
                acc[...] += z_in[m, t].astype(f32)

        h = m % HK
        if m < HK:
            dv_all[h // 2, grp, :, (h % 2) * DH : (h % 2 + 1) * DH] = acc[...].astype(bf16)
        else:
            dkey[:, h * DH : (h + 1) * DH] = acc[...].astype(bf16)

    def spread(part):
        mine = dv_all.at[part, grp]
        to_y = start(remote(mine, mine, d_send.at[part, 0], d_recv.at[part, 0], leaf, y_peer))
        to_c = start(remote(mine, mine, d_send.at[part, 1], d_recv.at[part, 1], leaf, c_peer))
        return to_y, to_c

    def relay(part, to_y):
        to_y.wait_recv()
        theirs = dv_all.at[part, y_peer]
        return start(remote(theirs, theirs, d_send.at[part, 2], d_recv.at[part, 2], leaf, c_peer))

    def partials(part, side):
        total = nn(hidden_t[grp, side].reshape(nz * rows, seg), dv_all[part, grp])
        for d in range(1, n_grp):
            owner = lax.rem(grp + n_grp - d, n_grp)
            total = total + nn(hid_all[d, side].reshape(nz * rows, seg), dv_all[part, owner])
        return total

    def px_copy(part):
        return remote(px_out.at[part], px_in.at[part], px_send.at[part], px_recv.at[part], x_peer, grp)

    def weight_x(part):
        total = partials(part, 1 - x).astype(bf16)
        px_out[part] = total.reshape(nz, rows, half)
        start(px_copy(part))
        pz_out[part] = partials(part, x).reshape(nz, rows, half)

    def weight_z(part):
        px_copy(part).wait_recv()
        copies = []
        for d in range(1, nz):
            t = lax.rem(z + d, nz)
            px_out_z = pz_out[part, t] + px_in[part, t].astype(f32)
            pz_in[part, 0, d - 1] = px_out_z.astype(bf16)
            copies.append(
                start(
                    remote(
                        pz_in.at[part, 0, d - 1], pz_in.at[part, 1, d - 1],
                        pz_send.at[part, d - 1], pz_recv.at[part, d - 1], t * NX + x, grp,
                    )
                )
            )
        return copies

    for h in range(HK):
        softmax(h)
        forward(h)
    for h in range(HK):
        gradients(h)
        x_stage(h)
        if h > 0:
            z_stage(h - 1)
    z_stage(HK - 1)
    for h in range(HK):
        x_stage(HK + h)
    owned(0)
    owned(1)
    to_y, to_c = spread(0)
    for copy in hidden:
        copy.wait_recv()
    relayed = relay(0, to_y)
    z_stage(HK)
    to_c.wait_recv()
    relayed.wait_recv()
    weight_x(0)
    owned(2)
    owned(3)
    to_y, to_c = spread(1)
    z_stage(HK + 1)
    relayed = relay(1, to_y)
    z_stage(HK + 2)
    to_c.wait_recv()
    relayed.wait_recv()
    weight_x(1)
    z_stage(HK + 3)
    copies = weight_z(0)
    width = hidden_ref.shape[1] // 4
    weight = jnp.concatenate([w_all[i].reshape(hidden_ref.shape[1], quarter) for i in range(4)], axis=1)
    dv_low = jnp.concatenate([dv_all[0, grp], dv_all[1, grp]], axis=1)
    for i in range(4):
        dhidden[:, i * width : (i + 1) * width] = nt(dv_low, weight[i * width : (i + 1) * width, :]).astype(bf16)
    copies += weight_z(1)
    for h in range(HK):
        owned(HK + h)
    for copy in copies:
        copy.wait_recv()
    for part in range(2):
        total = pz_out[part, z] + px_in[part, z].astype(f32)
        for d in range(1, nz):
            total = total + pz_in[part, 1, d - 1].astype(f32)
        dweight[:, part * half : (part + 1) * half] = total

    for h in range(HK):
        up, across = k_sems(h)
        sent(keys[h].at[leaf], keys[h], up, across)
        up, across = v_sems(h)
        sent(values[h].at[leaf], values[h], up, across)
    for m in range(2 * HK):
        for t in range(nz):
            @pl.when((t < z) | ((t == z) & (x == 1)))
            def _(t=t, m=m):
                x_copy(m, t).wait_send()
        for t in range(nz - 1):
            @pl.when(t < z)
            def _(t=t, m=m):
                z_copy(m, t).wait_send()
    for copy in pending:
        copy.wait_send()
    for h in range(HK):
        for store in stores(h):
            store.wait()


def hand_over_kernel(*refs):
    sems = refs[10]
    copies = [pltpu.make_async_copy(refs[i], refs[5 + i], sems.at[i]) for i in range(2, 5)]
    half = refs[0].shape[0] // 2
    for i in range(2):
        for j in range(2):
            rows = pl.ds(j * half, half)
            sem = sems.at[i if j == 0 else 5 + i]
            copies.append(pltpu.make_async_copy(refs[i].at[rows], refs[5 + i].at[rows], sem))
    for copy in copies:
        copy.start()
    for copy in copies:
        copy.wait()


def hand_over(*arrays):
    anywhere = pl.BlockSpec(memory_space=pl.ANY)
    return pl.pallas_call(
        hand_over_kernel,
        out_shape=[jax.ShapeDtypeStruct(a.shape, a.dtype) for a in arrays],
        in_specs=[anywhere] * 5,
        out_specs=[anywhere] * 5,
        scratch_shapes=[pltpu.SemaphoreType.DMA((7,))],
        compiler_params=pltpu.CompilerParams(vmem_limit_bytes=VMEM_LIMIT),
    )(*arrays)


def fast_shards(n_leaf, n_grp, hidden_states, query_rows, key_rows, value_weight, parent_links, out_grad):
    hidden, q, g, key = hidden_states[0], query_rows[0], out_grad[0], key_rows[0]
    rows, width = value_weight.shape
    seg, features = hidden.shape
    nz, ny = n_leaf // NX, n_grp // NC
    half = width // 2
    bf16, f32 = jnp.bfloat16, jnp.float32
    vmem = pl.BlockSpec(memory_space=pltpu.VMEM)
    anywhere = pl.BlockSpec(memory_space=pl.ANY)
    held, dma = pltpu.VMEM, pltpu.SemaphoreType.DMA
    pairs = lambda *dims: [dma(dims)] * 2
    out, dq, dkey, dhidden, dweight = pl.pallas_call(
        functools.partial(tree_kernel, n_leaf, n_grp),
        out_shape=[
            jax.ShapeDtypeStruct(q.shape, bf16),
            jax.ShapeDtypeStruct(q.shape, bf16),
            jax.ShapeDtypeStruct(key.shape, bf16),
            jax.ShapeDtypeStruct(hidden.shape, bf16),
            jax.ShapeDtypeStruct(value_weight.shape, f32),
        ],
        in_specs=[pl.BlockSpec(memory_space=pltpu.SMEM)] + [vmem] * 3 + [anywhere] * 2,
        out_specs=[anywhere] * 2 + [vmem] * 3,
        scratch_shapes=[
            held(q.shape, bf16),
            held(q.shape, bf16),
            held(q.shape, bf16),
            held(q.shape, bf16),
            held((n_grp, NX, nz, rows, seg), bf16),
            held((4, nz, NX, ny, NC, rows, width // 4), bf16),
        ]
        + [held((n_leaf, seg, DH), bf16)] * (2 * HK)
        + [
            held((n_leaf, 8, 128), jnp.int32),
            held((8, 128), jnp.int32),
            pltpu.SMEM((n_leaf, 128), jnp.int32),
            held((4 * seg, 2 * seg), f32),
            held((HQ // 2, 4 * seg, 2 * seg), f32),
            held((2 * HK, 4, seg, DH), bf16),
        ]
        + [held((2 * HK, nz, seg, DH), bf16)] * 4
        + [
            held((seg, DH), f32),
            held((n_grp, NX, nz, rows, seg), bf16),
            held((2, n_grp, seg, half), bf16),
            held((2, nz, rows, half), bf16),
            held((2, nz, rows, half), bf16),
            held((2, nz, rows, half), f32),
            held((2, 2, nz - 1, rows, half), bf16),
            dma((3,)),
            dma((HK, 2)),
        ]
        + pairs(n_leaf - 1)
        + pairs(2, nz - 1)
        + pairs(2, 4)
        + pairs(2, 5)
        + pairs(HK, nz - 1)
        + pairs(HK, nz)
        + pairs(HK, nz - 1)
        + pairs(HK, nz)
        + pairs(2 * HK, nz) * 2
        + pairs(n_grp - 1)
        + pairs(2, 3)
        + pairs(2)
        + pairs(2, nz - 1),
        compiler_params=pltpu.CompilerParams(
            collective_id=0, has_side_effects=True, vmem_limit_bytes=VMEM_LIMIT
        ),
        cost_estimate=pl.CostEstimate(
            flops=12 * HQ * seg * 4 * seg * DH + 6 * seg * features * width,
            bytes_accessed=10000000,
            transcendentals=HQ * seg * 4 * seg,
        ),
    )(parent_links, value_weight, key, hidden, q, g)
    out, dq, dkey, dhidden, dweight = hand_over(out, dq, dkey, dhidden, dweight)
    return out[None], dq[None], dkey[None], dhidden[None], dweight


def chain_slots(parent_list, own_index):
    total = parent_list.shape[0]

    def parent_of(node_index):
        hit = jnp.arange(total, dtype=jnp.int32) == node_index
        found = jnp.sum(jnp.where(hit, parent_list, 0))
        return jnp.where(node_index >= 0, found, -1)

    first = parent_of(own_index)
    second = parent_of(first)
    third = parent_of(second)
    return jnp.stack([first, second, third])


def key_mask(ancestors, segment_len):
    valid = jnp.concatenate([ancestors >= 0, jnp.ones((1,), bool)])
    block_ok = jnp.repeat(valid, segment_len)[None, :]
    row_ids = jnp.arange(segment_len, dtype=jnp.int32)[:, None]
    col_ids = jnp.arange(4 * segment_len, dtype=jnp.int32)[None, :]
    causal = (col_ids < 3 * segment_len) | (col_ids - 3 * segment_len <= row_ids)
    return block_ok & causal


def segment_pass(query_seg, key_all, value_all, grad_seg, visible):
    segment_len = query_seg.shape[0]
    groups = HQ // HK
    scale_factor = 1.0 / DH**0.5
    query_heads = query_seg.reshape(segment_len, HK, groups, DH)
    key_heads = key_all.reshape(-1, HK, DH)
    value_heads = value_all.reshape(-1, HK, DH)
    grad_heads = grad_seg.reshape(segment_len, HK, groups, DH)
    scores = (
        jnp.einsum("rhgd,khd->hgrk", query_heads, key_heads, preferred_element_type=jnp.float32)
        * scale_factor
    )
    scores = jnp.where(visible, scores, -1e30)
    row_max = jnp.max(scores, axis=-1, keepdims=True)
    weights_exp = jnp.where(visible, jnp.exp(scores - row_max), 0.0)
    probs = weights_exp / jnp.sum(weights_exp, axis=-1, keepdims=True)
    probs_low = probs.astype(jnp.bfloat16)
    output = jnp.einsum(
        "hgrk,khd->rhgd", probs_low, value_heads, preferred_element_type=jnp.float32
    )
    output = output.reshape(segment_len, HQ * DH).astype(jnp.bfloat16)
    dprobs = jnp.einsum(
        "rhgd,khd->hgrk", grad_heads, value_heads, preferred_element_type=jnp.float32
    )
    delta = jnp.sum(probs * dprobs, axis=-1, keepdims=True)
    dscores = (probs * (dprobs - delta)).astype(jnp.bfloat16)
    query_grad = (
        jnp.einsum("hgrk,khd->rhgd", dscores, key_heads, preferred_element_type=jnp.float32)
        * scale_factor
    )
    query_grad = query_grad.reshape(segment_len, HQ * DH).astype(jnp.bfloat16)
    key_part = (
        jnp.einsum("hgrk,rhgd->khd", dscores, query_heads, preferred_element_type=jnp.float32)
        * scale_factor
    )
    value_part = jnp.einsum(
        "hgrk,rhgd->khd", probs_low, grad_heads, preferred_element_type=jnp.float32
    )
    grad_term = jnp.concatenate(
        [key_part.reshape(-1, HK * DH), value_part.reshape(-1, HK * DH)], axis=1
    )
    return (output, query_grad, grad_term)


def shards(hidden_states, query_rows, key_rows, value_weight, parent_links, out_grad):
    hidden_local = hidden_states[0]
    query_local = query_rows[0]
    key_local = key_rows[0]
    grad_local = out_grad[0]
    segment_len = hidden_local.shape[0]
    key_width = key_local.shape[1]
    parent_list = lax.all_gather(parent_links, "leaf", axis=1, tiled=True)[0]
    own_index = lax.axis_index("leaf")
    ancestors = chain_slots(parent_list, own_index)
    columns = hidden_local
    values = jnp.dot(
        columns,
        lax.all_gather(value_weight, ("leaf", "grp"), axis=0, tiled=True),
        preferred_element_type=jnp.float32,
    )
    values = values.astype(jnp.bfloat16)
    key_value = jnp.concatenate([key_local, values], axis=1)
    every_segment = lax.all_gather(key_value, "leaf", axis=0, tiled=True)
    fetched = jnp.concatenate(
        [
            lax.dynamic_slice_in_dim(
                every_segment, jnp.maximum(ancestors[i], 0) * segment_len, segment_len, 0
            )
            for i in range(3)
        ],
        axis=0,
    )
    gathered = jnp.concatenate([fetched, key_value], axis=0)
    output, query_grad, grad_term = segment_pass(
        query_local,
        gathered[:, :key_width],
        gathered[:, key_width:],
        grad_local,
        key_mask(ancestors, segment_len),
    )
    grad_low = grad_term.astype(jnp.bfloat16)
    owners = jnp.concatenate([ancestors, own_index[None]])
    grad_wide = grad_low.astype(jnp.float32)
    targets = (
        owners[:, None] * segment_len + jnp.arange(segment_len, dtype=jnp.int32)[None, :]
    ).reshape(-1)
    keep_rows = (
        jnp.repeat(owners >= 0, segment_len)
        & (targets >= 0)
        & (targets < segment_len * lax.axis_size("leaf"))
    )
    targets = jnp.where(keep_rows, targets, segment_len * lax.axis_size("leaf"))
    sums = lax.psum_scatter(
        jnp.zeros((segment_len * lax.axis_size("leaf"), grad_wide.shape[1]), grad_wide.dtype)
        .at[targets]
        .add(grad_wide, mode="drop")
        .astype(jnp.bfloat16),
        "leaf",
        scatter_dimension=0,
        tiled=True,
    ).astype(jnp.float32)
    key_grad = sums[:, :key_width].astype(jnp.bfloat16)
    value_grad = sums[:, key_width:].astype(jnp.bfloat16)
    columns = hidden_local
    weight_grad = lax.psum_scatter(
        lax.dot_general(
            columns, value_grad, (((0,), (0,)), ((), ())), preferred_element_type=jnp.float32
        ),
        ("leaf", "grp"),
        scatter_dimension=0,
        tiled=True,
    )
    hidden_grad = lax.dot_general(
        value_grad,
        lax.all_gather(value_weight, ("leaf", "grp"), axis=0, tiled=True),
        (((1,), (1,)), ((), ())),
        preferred_element_type=jnp.float32,
    )
    hidden_grad = hidden_grad.astype(jnp.bfloat16)
    return (output[None], query_grad[None], key_grad[None], hidden_grad[None], weight_grad)


def solution(mesh):
    placed = (
        P("grp", "leaf", None),
        P("grp", "leaf", None),
        P("grp", "leaf", None),
        P(("leaf", "grp"), None),
        P("grp", "leaf"),
        P("grp", "leaf", None),
    )
    n_leaf, n_grp = mesh.shape["leaf"], mesh.shape["grp"]

    def body(hidden_states, query_rows, key_rows, value_weight, parent_links, out_grad):
        args = (hidden_states, query_rows, key_rows, value_weight, parent_links, out_grad)
        if n_leaf % NX == 0 and n_grp == 2 * NC and value_weight.shape[0] % 16 == 0:
            return fast_shards(n_leaf, n_grp, *args)
        return shards(*args)

    return jax.shard_map(
        body,
        mesh=mesh,
        in_specs=placed,
        out_specs=(
            P("grp", "leaf", None),
            P("grp", "leaf", None),
            P("grp", "leaf", None),
            P("grp", "leaf", None),
            P(("leaf", "grp"), None),
        ),
        check_vma=False,
    )
```

```python
import functools

import jax
import jax.numpy as jnp
from jax import lax
from jax.experimental import pallas as pl
from jax.experimental.pallas import tpu as pltpu
from jax.sharding import PartitionSpec as P

HQ = 40
HK = 4
DH = 128
MESH = pl.DeviceIdType.MESH
NX = 2
NC = 2
VMEM_LIMIT = 56 * 1024 * 1024


def nt(a, b):
    return lax.dot_general(a, b, (((1,), (1,)), ((), ())), preferred_element_type=jnp.float32)


def nn(a, b):
    return jnp.dot(a, b, preferred_element_type=jnp.float32)


def place():
    leaf = lax.axis_index("leaf")
    grp = lax.axis_index("grp")
    return leaf, grp, leaf // NX, leaf % NX, grp // NC, grp % NC


def remote(src, dst, send, recv, leaf, grp):
    return pltpu.make_async_remote_copy(
        src_ref=src,
        dst_ref=dst,
        send_sem=send,
        recv_sem=recv,
        device_id=(leaf, grp),
        device_id_type=MESH,
    )


def greet(leaf, grp, n_leaf, n_grp):
    barrier = pltpu.get_barrier_semaphore()
    for step in range(1, n_leaf):
        pl.semaphore_signal(
            barrier, inc=1, device_id=(lax.rem(leaf + step, n_leaf), grp), device_id_type=MESH
        )
    for step in range(1, n_grp):
        pl.semaphore_signal(
            barrier, inc=1, device_id=(leaf, lax.rem(grp + step, n_grp)), device_id_type=MESH
        )
    pl.semaphore_wait(barrier, n_leaf + n_grp - 2)


def ancestors_of(par, own):
    first = par[own, 0]
    second = jnp.where(first >= 0, par[jnp.maximum(first, 0), 0], -1)
    third = jnp.where(second >= 0, par[jnp.maximum(second, 0), 0], -1)
    return first, second, third


def tree_kernel(
    n_leaf, n_grp,
    parent_ref, w_ref, key_ref, hidden_ref, q_hbm, g_hbm,
    out_hbm, dq_hbm, dkey, dhidden, dweight,
    q_ref, g_ref, out_ref, dq_ref, hidden_t, w_all, k0, k1, v0, v1, parents, own_parent, par, bias, probs, terms,
    x_out, x_in, z_out, z_in, acc, hid_all, dv_all, px_out, px_in, pz_out, pz_in,
    load_sem, store_sem, par_send, par_recv, wz_send, wz_recv, w_send, w_recv, c_send, c_recv,
    kz_send, kz_recv, kx_send, kx_recv, vz_send, vz_recv, vx_send, vx_recv,
    gx_send, gx_recv, gz_send, gz_recv, h_send, h_recv, d_send, d_recv,
    px_send, px_recv, pz_send, pz_recv,
):
    leaf, grp, z, x, y, c = place()
    nz = n_leaf // NX
    seg = key_ref.shape[0]
    f32, bf16 = jnp.float32, jnp.bfloat16
    scale = 1.0 / DH**0.5
    fold = scale * 1.4426950408889634
    x_peer, y_peer, c_peer = z * NX + (1 - x), (1 - y) * NC + c, y * NC + (1 - c)
    keys, values = (k0, k1), (v0, v1)
    half = w_ref.shape[1] // 2
    spot = x * nz + z
    pending = []

    loads = [
        pltpu.make_async_copy(q_hbm, q_ref, load_sem.at[0]),
        pltpu.make_async_copy(g_hbm, g_ref, load_sem.at[1]),
    ]
    for load in loads:
        load.start()
    own_parent[...] = jnp.full(own_parent.shape, parent_ref[0, 0], jnp.int32)
    greet(leaf, grp, n_leaf, n_grp)

    def start(copy):
        copy.start()
        pending.append(copy)
        return copy

    def w_over_z(part):
        copies = []
        two = pl.ds(2 * part, 2)
        for d in range(1, nz):
            copies.append(
                start(
                    remote(
                        w_all.at[two, z, x, y, c], w_all.at[two, z, x, y, c],
                        wz_send.at[part, d - 1], wz_recv.at[part, d - 1], lax.rem(z + d, nz) * NX + x, grp,
                    )
                )
            )
        return copies

    quarter = half // 2
    for i in range(4):
        w_all[i, z, x, y, c] = w_ref[:, i * quarter : (i + 1) * quarter]
    wz = w_over_z(0)
    links = []
    for d in range(1, n_leaf):
        to = lax.rem(leaf + d, n_leaf)
        links.append(
            start(remote(own_parent, parents.at[leaf], par_send.at[d - 1], par_recv.at[d - 1], to, grp))
        )
    for part in range(2):
        keys[part][spot] = key_ref[:, part * half : (part + 1) * half]
    parents[leaf] = own_parent[...]

    def up_copy(whole, sems, part, d):
        block = whole[part].at[spot]
        return remote(block, block, sems[0].at[part, d - 1], sems[1].at[part, d - 1], leaf + d * NX, grp)

    def up_start(whole, sems, part):
        for d in range(1, nz):
            @pl.when(z + d < nz)
            def _(d=d):
                up_copy(whole, sems, part, d).start()

    def across_copy(whole, sems, part, k, column):
        blocks = whole[part].at[pl.ds(column * nz, k + 1)]
        return remote(blocks, blocks, sems[2].at[part], sems[3].at[part], x_peer, grp)

    def across_start(whole, sems, part):
        for d in range(1, nz):
            @pl.when(z - d >= 0)
            def _(d=d):
                block = whole[part].at[spot - d]
                remote(block, block, sems[0].at[part, d - 1], sems[1].at[part, d - 1], leaf, grp).wait_recv()

        for k in range(nz):
            @pl.when(z == k)
            def _(k=k):
                across_copy(whole, sems, part, k, x).start()

    def across_ready(whole, sems, part):
        for k in range(nz):
            @pl.when(z == k)
            def _(k=k):
                across_copy(whole, sems, part, k, 1 - x).wait_recv()

    def sent(whole, sems, part):
        for d in range(1, nz):
            @pl.when(z + d < nz)
            def _(d=d):
                up_copy(whole, sems, part, d).wait_send()

        for k in range(nz):
            @pl.when(z == k)
            def _(k=k):
                across_copy(whole, sems, part, k, x).wait_send()

    k_sems = (kz_send, kz_recv, kx_send, kx_recv)
    v_sems = (vz_send, vz_recv, vx_send, vx_recv)

    rows = hidden_t.shape[3]
    for first in range(nz):
        block = NX * n_grp * rows
        turned = hidden_ref[:, first * block : (first + 1) * block].T
        for i in range(NX):
            for j in range(n_grp):
                at = (i * n_grp + j) * rows
                hidden_t[j, i, first] = turned[at : at + rows]

    to_core = [[], []]

    def w_copy(part, i, block, leaf_to, grp_to):
        return start(remote(block, block, w_send.at[part, i], w_recv.at[part, i], leaf_to, grp_to))

    def w_core(part, i, block):
        to_core[part].append(
            start(remote(block, block, c_send.at[part, i], c_recv.at[part, i], leaf, c_peer))
        )

    def w_first(part):
        a, b = 2 * part, 2 * part + 1
        return (
            w_copy(part, 0, w_all.at[a, :, x, y, c], x_peer, grp),
            w_copy(part, 1, w_all.at[b, :, x, y, c], leaf, y_peer),
        )

    def w_second(part, first):
        a, b = 2 * part, 2 * part + 1
        first[0].wait_recv()
        over_y = w_copy(part, 2, w_all.at[a, :, :, y, c], leaf, y_peer)
        first[1].wait_recv()
        over_x = w_copy(part, 3, w_all.at[b, :, x, :, c], x_peer, grp)
        w_core(part, 0, w_all.at[pl.ds(2 * part, 2), :, x, y, c])
        w_core(part, 1, w_all.at[a, :, 1 - x, y, c])
        w_core(part, 2, w_all.at[b, :, x, 1 - y, c])
        return over_y, over_x

    def w_third(part, second):
        a, b = 2 * part, 2 * part + 1
        second[0].wait_recv()
        w_core(part, 3, w_all.at[a, :, :, 1 - y, c])
        second[1].wait_recv()
        w_core(part, 4, w_all.at[b, :, 1 - x, :, c])

    def project(part):
        for copy in to_core[part]:
            copy.wait_recv()
        weight = jnp.concatenate(
            [w_all[2 * part + i].reshape(hidden_ref.shape[1], quarter) for i in range(2)], axis=1
        )
        pair = nn(hidden_ref[...], weight).astype(bf16)
        values[part][spot] = pair
        up_start(values, v_sems, part)

    for copy in wz:
        copy.wait_recv()
    first0 = w_first(0)
    wz = w_over_z(1)
    second0 = w_second(0, first0)
    for copy in wz:
        copy.wait_recv()
    first1 = w_first(1)
    for part in range(2):
        up_start(keys, k_sems, part)
    w_third(0, second0)
    second1 = w_second(1, first1)
    project(0)
    across_start(keys, k_sems, 0)
    w_third(1, second1)
    hidden = []
    for d in range(1, n_grp):
        to = lax.rem(grp + d, n_grp)
        hidden.append(
            start(remote(hidden_t.at[to], hid_all.at[d], h_send.at[d - 1], h_recv.at[d - 1], leaf, to))
        )
    project(1)
    across_start(keys, k_sems, 1)
    for copy in links:
        copy.wait_recv()
    listing = pltpu.make_async_copy(parents.at[:, 0], par, load_sem.at[2])
    listing.start()

    listing.wait()
    chain = ancestors_of(par, leaf)
    for i in range(3):
        bias[i * seg : (i + 1) * seg, :] = jnp.full(
            (seg, 2 * seg), jnp.where(chain[i] >= 0, 0.0, -1e30), f32
        )
    col = lax.broadcasted_iota(jnp.int32, (seg, 2 * seg), 0)
    row = lax.broadcasted_iota(jnp.int32, (seg, 2 * seg), 1)
    row = jnp.where(row >= seg, row - seg, row)
    bias[3 * seg :, :] = jnp.where(col <= row, 0.0, -1e30)
    for load in loads:
        load.wait()

    groups = HQ // HK
    above = [jnp.maximum(chain[i], 0) for i in range(3)]
    slots = [lax.rem(a, NX) * nz + lax.div(a, NX) for a in above] + [spot]

    def lanes_in(h):
        return slice(h % 2 * DH, (h % 2 + 1) * DH)

    def places(h, pair):
        at = (h * groups + 2 * pair) * DH
        return slice(at, at + DH), slice(at + DH, at + 2 * DH)

    def keys_of(h):
        return jnp.concatenate([keys[h // 2][slot, :, lanes_in(h)] for slot in slots], axis=0)

    def softmax(h):
        if h % 2 == 0:
            across_ready(keys, k_sems, h // 2)
        key = keys_of(h)
        for pair in range(groups // 2):
            one, two = places(h, pair)
            q = jnp.concatenate([q_ref[:, one], q_ref[:, two]], axis=0)
            s = nt(key, q) * fold + bias[...]
            e = jnp.exp2(s - jnp.max(s, axis=0, keepdims=True))
            probs[h * (groups // 2) + pair] = e * (1.0 / jnp.sum(e, axis=0, keepdims=True))

    def stores(h):
        lanes = pl.ds(h * groups * DH, groups * DH)
        return (
            pltpu.make_async_copy(out_ref.at[:, lanes], out_hbm.at[:, lanes], store_sem.at[h, 0]),
            pltpu.make_async_copy(dq_ref.at[:, lanes], dq_hbm.at[:, lanes], store_sem.at[h, 1]),
        )

    def gradients(h):
        if h % 2 == 0:
            across_ready(values, v_sems, h // 2)
        value = jnp.concatenate([values[h // 2][slot, :, lanes_in(h)] for slot in slots], axis=0)
        key_t = keys_of(h).T
        value_t = value.T
        dk = jnp.zeros((4 * seg, DH), f32)
        dv = jnp.zeros((4 * seg, DH), f32)
        for pair in range(groups // 2):
            one, two = places(h, pair)
            q = jnp.concatenate([q_ref[:, one], q_ref[:, two]], axis=0)
            g = jnp.concatenate([g_ref[:, one], g_ref[:, two]], axis=0)
            p = probs[h * (groups // 2) + pair]
            p_low = p.astype(bf16)
            dp = nt(value, g)
            delta = jnp.sum(p * dp, axis=0, keepdims=True)
            ds = (p * (dp - delta)).astype(bf16)
            o = nn(value_t, p_low).T.astype(bf16)
            out_ref[:, one] = o[:seg]
            out_ref[:, two] = o[seg:]
            dq = (nn(key_t, ds) * scale).T.astype(bf16)
            dq_ref[:, one] = dq[:seg]
            dq_ref[:, two] = dq[seg:]
            dk = dk + nn(ds, q)
            dv = dv + nn(p_low, g)
        for store in stores(h):
            store.start()
        for i in range(4):
            terms[h // 2, i, :, lanes_in(h)] = dv[i * seg : (i + 1) * seg].astype(bf16)
            terms[2 + h // 2, i, :, lanes_in(h)] = (dk[i * seg : (i + 1) * seg] * scale).astype(bf16)

    def term(m, target):
        slot = jnp.where(chain[0] == target, 0, jnp.where(chain[1] == target, 1, 2))
        hit = (chain[0] == target) | (chain[1] == target) | (chain[2] == target)
        block = terms[m, slot]
        return jnp.where(hit, block, jnp.zeros_like(block))

    def x_copy(m, k):
        blocks = pl.ds(0, k + 1)
        return remote(x_out.at[m, blocks], x_in.at[m, blocks], gx_send.at[m], gx_recv.at[m], x_peer, grp)

    def z_copy(m, t):
        return remote(z_out.at[m, t], z_in.at[m, z], gz_send.at[m, t], gz_recv.at[m, z], t * NX + x, grp)

    def x_stage(m):
        for k in range(nz):
            @pl.when(z == k)
            def _(k=k):
                for t in range(k + 1):
                    x_out[m, t] = term(m, t * NX + (1 - x))
                x_copy(m, k).start()

    def z_stage(m):
        for k in range(nz):
            @pl.when(z == k)
            def _(k=k):
                x_copy(m, k).wait_recv()
                for t in range(k):
                    total = term(m, t * NX + x).astype(f32) + x_in[m, t].astype(f32)
                    z_out[m, t] = total.astype(bf16)
                    z_copy(m, t).start()

    def owned(m):
        acc[...] = terms[m, 3].astype(f32) + x_in[m, z].astype(f32)
        for t in range(1, nz):
            @pl.when(t > z)
            def _(t=t):
                block = z_in.at[m, t]
                remote(block, block, gz_send.at[m, t], gz_recv.at[m, t], t * NX + x, grp).wait_recv()
                acc[...] += z_in[m, t].astype(f32)

        if m < 2:
            dv_all[m, grp] = acc[...].astype(bf16)
        else:
            dkey[:, (m - 2) * half : (m - 1) * half] = acc[...].astype(bf16)

    def spread(part):
        mine = dv_all.at[part, grp]
        to_y = start(remote(mine, mine, d_send.at[part, 0], d_recv.at[part, 0], leaf, y_peer))
        to_c = start(remote(mine, mine, d_send.at[part, 1], d_recv.at[part, 1], leaf, c_peer))
        return to_y, to_c

    def relay(part, to_y):
        to_y.wait_recv()
        theirs = dv_all.at[part, y_peer]
        return start(remote(theirs, theirs, d_send.at[part, 2], d_recv.at[part, 2], leaf, c_peer))

    def partials(part, side):
        total = nn(hidden_t[grp, side].reshape(nz * rows, seg), dv_all[part, grp])
        for d in range(1, n_grp):
            owner = lax.rem(grp + n_grp - d, n_grp)
            total = total + nn(hid_all[d, side].reshape(nz * rows, seg), dv_all[part, owner])
        return total

    def px_copy(part):
        return remote(px_out.at[part], px_in.at[part], px_send.at[part], px_recv.at[part], x_peer, grp)

    def weight_x(part):
        total = partials(part, 1 - x).astype(bf16)
        px_out[part] = total.reshape(nz, rows, half)
        start(px_copy(part))
        pz_out[part] = partials(part, x).reshape(nz, rows, half)

    def weight_z(part):
        px_copy(part).wait_recv()
        copies = []
        for d in range(1, nz):
            t = lax.rem(z + d, nz)
            px_out_z = pz_out[part, t] + px_in[part, t].astype(f32)
            pz_in[part, 0, d - 1] = px_out_z.astype(bf16)
            copies.append(
                start(
                    remote(
                        pz_in.at[part, 0, d - 1], pz_in.at[part, 1, d - 1],
                        pz_send.at[part, d - 1], pz_recv.at[part, d - 1], t * NX + x, grp,
                    )
                )
            )
        return copies

    softmax(0)
    across_start(values, v_sems, 0)
    softmax(1)
    across_start(values, v_sems, 1)
    softmax(2)
    softmax(3)
    gradients(0)
    gradients(1)
    x_stage(0)
    gradients(2)
    gradients(3)
    x_stage(1)
    z_stage(0)
    x_stage(2)
    owned(0)
    to_y, to_c = spread(0)
    z_stage(1)
    x_stage(3)
    for copy in hidden:
        copy.wait_recv()
    relayed = relay(0, to_y)
    to_c.wait_recv()
    relayed.wait_recv()
    weight_x(0)
    owned(1)
    to_y, to_c = spread(1)
    z_stage(2)
    relayed = relay(1, to_y)
    to_c.wait_recv()
    relayed.wait_recv()
    weight_x(1)
    z_stage(3)
    copies = weight_z(0)
    width = hidden_ref.shape[1] // 4
    weight = jnp.concatenate([w_all[i].reshape(hidden_ref.shape[1], quarter) for i in range(4)], axis=1)
    dv_low = jnp.concatenate([dv_all[0, grp], dv_all[1, grp]], axis=1)
    for i in range(4):
        dhidden[:, i * width : (i + 1) * width] = nt(dv_low, weight[i * width : (i + 1) * width, :]).astype(bf16)
    copies += weight_z(1)
    owned(2)
    owned(3)
    for copy in copies:
        copy.wait_recv()
    for part in range(2):
        total = pz_out[part, z] + px_in[part, z].astype(f32)
        for d in range(1, nz):
            total = total + pz_in[part, 1, d - 1].astype(f32)
        dweight[:, part * half : (part + 1) * half] = total

    for part in range(2):
        sent(keys, k_sems, part)
        sent(values, v_sems, part)
    for m in range(4):
        for k in range(nz):
            @pl.when(z == k)
            def _(k=k, m=m):
                x_copy(m, k).wait_send()
                for t in range(k):
                    z_copy(m, t).wait_send()
    for copy in pending:
        copy.wait_send()
    for h in range(HK):
        for store in stores(h):
            store.wait()


def hand_over_kernel(*refs):
    for i in range(5):
        refs[5 + i][...] = refs[i][...]


def hand_over(*arrays):
    blocks = [pl.BlockSpec((a.shape[0], a.shape[1] // HK), lambda i: (0, i)) for a in arrays]
    return pl.pallas_call(
        hand_over_kernel,
        out_shape=[jax.ShapeDtypeStruct(a.shape, a.dtype) for a in arrays],
        grid=(HK,),
        in_specs=blocks,
        out_specs=blocks,
        compiler_params=pltpu.CompilerParams(vmem_limit_bytes=VMEM_LIMIT),
    )(*arrays)


def fast_shards(n_leaf, n_grp, hidden_states, query_rows, key_rows, value_weight, parent_links, out_grad):
    hidden, q, g, key = hidden_states[0], query_rows[0], out_grad[0], key_rows[0]
    rows, width = value_weight.shape
    seg, features = hidden.shape
    nz, ny = n_leaf // NX, n_grp // NC
    half = width // 2
    bf16, f32 = jnp.bfloat16, jnp.float32
    vmem = pl.BlockSpec(memory_space=pltpu.VMEM)
    anywhere = pl.BlockSpec(memory_space=pl.ANY)
    held, dma = pltpu.VMEM, pltpu.SemaphoreType.DMA
    pairs = lambda *dims: [dma(dims)] * 2
    out, dq, dkey, dhidden, dweight = pl.pallas_call(
        functools.partial(tree_kernel, n_leaf, n_grp),
        out_shape=[
            jax.ShapeDtypeStruct(q.shape, bf16),
            jax.ShapeDtypeStruct(q.shape, bf16),
            jax.ShapeDtypeStruct(key.shape, bf16),
            jax.ShapeDtypeStruct(hidden.shape, bf16),
            jax.ShapeDtypeStruct(value_weight.shape, f32),
        ],
        in_specs=[pl.BlockSpec(memory_space=pltpu.SMEM)] + [vmem] * 3 + [anywhere] * 2,
        out_specs=[anywhere] * 2 + [vmem] * 3,
        scratch_shapes=[
            held(q.shape, bf16),
            held(q.shape, bf16),
            held(q.shape, bf16),
            held(q.shape, bf16),
            held((n_grp, NX, nz, rows, seg), bf16),
            held((4, nz, NX, ny, NC, rows, width // 4), bf16),
        ]
        + [held((n_leaf, seg, half), bf16)] * 4
        + [
            held((n_leaf, 8, 128), jnp.int32),
            held((8, 128), jnp.int32),
            pltpu.SMEM((n_leaf, 128), jnp.int32),
            held((4 * seg, 2 * seg), f32),
            held((HQ // 2, 4 * seg, 2 * seg), f32),
            held((4, 4, seg, half), bf16),
        ]
        + [held((4, nz, seg, half), bf16)] * 4
        + [
            held((seg, half), f32),
            held((n_grp, NX, nz, rows, seg), bf16),
            held((2, n_grp, seg, half), bf16),
            held((2, nz, rows, half), bf16),
            held((2, nz, rows, half), bf16),
            held((2, nz, rows, half), f32),
            held((2, 2, nz - 1, rows, half), bf16),
            dma((3,)),
            dma((HK, 2)),
        ]
        + pairs(n_leaf - 1)
        + pairs(2, nz - 1)
        + pairs(2, 4)
        + pairs(2, 5)
        + (pairs(2, nz - 1) + pairs(2)) * 2
        + pairs(4)
        + pairs(4, nz)
        + pairs(n_grp - 1)
        + pairs(2, 3)
        + pairs(2)
        + pairs(2, nz - 1),
        compiler_params=pltpu.CompilerParams(
            collective_id=0, has_side_effects=True, vmem_limit_bytes=VMEM_LIMIT
        ),
        cost_estimate=pl.CostEstimate(
            flops=12 * HQ * seg * 4 * seg * DH + 6 * seg * features * width,
            bytes_accessed=10000000,
            transcendentals=HQ * seg * 4 * seg,
        ),
    )(parent_links, value_weight, key, hidden, q, g)
    out, dq, dkey, dhidden, dweight = hand_over(out, dq, dkey, dhidden, dweight)
    return out[None], dq[None], dkey[None], dhidden[None], dweight


def chain_slots(parent_list, own_index):
    total = parent_list.shape[0]

    def parent_of(node_index):
        hit = jnp.arange(total, dtype=jnp.int32) == node_index
        found = jnp.sum(jnp.where(hit, parent_list, 0))
        return jnp.where(node_index >= 0, found, -1)

    first = parent_of(own_index)
    second = parent_of(first)
    third = parent_of(second)
    return jnp.stack([first, second, third])


def key_mask(ancestors, segment_len):
    valid = jnp.concatenate([ancestors >= 0, jnp.ones((1,), bool)])
    block_ok = jnp.repeat(valid, segment_len)[None, :]
    row_ids = jnp.arange(segment_len, dtype=jnp.int32)[:, None]
    col_ids = jnp.arange(4 * segment_len, dtype=jnp.int32)[None, :]
    causal = (col_ids < 3 * segment_len) | (col_ids - 3 * segment_len <= row_ids)
    return block_ok & causal


def segment_pass(query_seg, key_all, value_all, grad_seg, visible):
    segment_len = query_seg.shape[0]
    groups = HQ // HK
    scale_factor = 1.0 / DH**0.5
    query_heads = query_seg.reshape(segment_len, HK, groups, DH)
    key_heads = key_all.reshape(-1, HK, DH)
    value_heads = value_all.reshape(-1, HK, DH)
    grad_heads = grad_seg.reshape(segment_len, HK, groups, DH)
    scores = (
        jnp.einsum("rhgd,khd->hgrk", query_heads, key_heads, preferred_element_type=jnp.float32)
        * scale_factor
    )
    scores = jnp.where(visible, scores, -1e30)
    row_max = jnp.max(scores, axis=-1, keepdims=True)
    weights_exp = jnp.where(visible, jnp.exp(scores - row_max), 0.0)
    probs = weights_exp / jnp.sum(weights_exp, axis=-1, keepdims=True)
    probs_low = probs.astype(jnp.bfloat16)
    output = jnp.einsum(
        "hgrk,khd->rhgd", probs_low, value_heads, preferred_element_type=jnp.float32
    )
    output = output.reshape(segment_len, HQ * DH).astype(jnp.bfloat16)
    dprobs = jnp.einsum(
        "rhgd,khd->hgrk", grad_heads, value_heads, preferred_element_type=jnp.float32
    )
    delta = jnp.sum(probs * dprobs, axis=-1, keepdims=True)
    dscores = (probs * (dprobs - delta)).astype(jnp.bfloat16)
    query_grad = (
        jnp.einsum("hgrk,khd->rhgd", dscores, key_heads, preferred_element_type=jnp.float32)
        * scale_factor
    )
    query_grad = query_grad.reshape(segment_len, HQ * DH).astype(jnp.bfloat16)
    key_part = (
        jnp.einsum("hgrk,rhgd->khd", dscores, query_heads, preferred_element_type=jnp.float32)
        * scale_factor
    )
    value_part = jnp.einsum(
        "hgrk,rhgd->khd", probs_low, grad_heads, preferred_element_type=jnp.float32
    )
    grad_term = jnp.concatenate(
        [key_part.reshape(-1, HK * DH), value_part.reshape(-1, HK * DH)], axis=1
    )
    return (output, query_grad, grad_term)


def shards(hidden_states, query_rows, key_rows, value_weight, parent_links, out_grad):
    hidden_local = hidden_states[0]
    query_local = query_rows[0]
    key_local = key_rows[0]
    grad_local = out_grad[0]
    segment_len = hidden_local.shape[0]
    key_width = key_local.shape[1]
    parent_list = lax.all_gather(parent_links, "leaf", axis=1, tiled=True)[0]
    own_index = lax.axis_index("leaf")
    ancestors = chain_slots(parent_list, own_index)
    columns = hidden_local
    values = jnp.dot(
        columns,
        lax.all_gather(value_weight, ("leaf", "grp"), axis=0, tiled=True),
        preferred_element_type=jnp.float32,
    )
    values = values.astype(jnp.bfloat16)
    key_value = jnp.concatenate([key_local, values], axis=1)
    every_segment = lax.all_gather(key_value, "leaf", axis=0, tiled=True)
    fetched = jnp.concatenate(
        [
            lax.dynamic_slice_in_dim(
                every_segment, jnp.maximum(ancestors[i], 0) * segment_len, segment_len, 0
            )
            for i in range(3)
        ],
        axis=0,
    )
    gathered = jnp.concatenate([fetched, key_value], axis=0)
    output, query_grad, grad_term = segment_pass(
        query_local,
        gathered[:, :key_width],
        gathered[:, key_width:],
        grad_local,
        key_mask(ancestors, segment_len),
    )
    grad_low = grad_term.astype(jnp.bfloat16)
    owners = jnp.concatenate([ancestors, own_index[None]])
    grad_wide = grad_low.astype(jnp.float32)
    targets = (
        owners[:, None] * segment_len + jnp.arange(segment_len, dtype=jnp.int32)[None, :]
    ).reshape(-1)
    keep_rows = (
        jnp.repeat(owners >= 0, segment_len)
        & (targets >= 0)
        & (targets < segment_len * lax.axis_size("leaf"))
    )
    targets = jnp.where(keep_rows, targets, segment_len * lax.axis_size("leaf"))
    sums = lax.psum_scatter(
        jnp.zeros((segment_len * lax.axis_size("leaf"), grad_wide.shape[1]), grad_wide.dtype)
        .at[targets]
        .add(grad_wide, mode="drop")
        .astype(jnp.bfloat16),
        "leaf",
        scatter_dimension=0,
        tiled=True,
    ).astype(jnp.float32)
    key_grad = sums[:, :key_width].astype(jnp.bfloat16)
    value_grad = sums[:, key_width:].astype(jnp.bfloat16)
    columns = hidden_local
    weight_grad = lax.psum_scatter(
        lax.dot_general(
            columns, value_grad, (((0,), (0,)), ((), ())), preferred_element_type=jnp.float32
        ),
        ("leaf", "grp"),
        scatter_dimension=0,
        tiled=True,
    )
    hidden_grad = lax.dot_general(
        value_grad,
        lax.all_gather(value_weight, ("leaf", "grp"), axis=0, tiled=True),
        (((1,), (1,)), ((), ())),
        preferred_element_type=jnp.float32,
    )
    hidden_grad = hidden_grad.astype(jnp.bfloat16)
    return (output[None], query_grad[None], key_grad[None], hidden_grad[None], weight_grad)


def solution(mesh):
    placed = (
        P("grp", "leaf", None),
        P("grp", "leaf", None),
        P("grp", "leaf", None),
        P(("leaf", "grp"), None),
        P("grp", "leaf"),
        P("grp", "leaf", None),
    )
    n_leaf, n_grp = mesh.shape["leaf"], mesh.shape["grp"]

    def body(hidden_states, query_rows, key_rows, value_weight, parent_links, out_grad):
        args = (hidden_states, query_rows, key_rows, value_weight, parent_links, out_grad)
        if n_leaf % NX == 0 and n_grp == 2 * NC and value_weight.shape[0] % 16 == 0:
            return fast_shards(n_leaf, n_grp, *args)
        return shards(*args)

    return jax.shard_map(
        body,
        mesh=mesh,
        in_specs=placed,
        out_specs=(
            P("grp", "leaf", None),
            P("grp", "leaf", None),
            P("grp", "leaf", None),
            P("grp", "leaf", None),
            P(("leaf", "grp"), None),
        ),
        check_vma=False,
    )
```
